256 devices in a mesh: rows: 16 (over x, y), cols: 16 (over z, core).
Axes of the slice: x: 4, y: 4, z: 8, core: 2. Of those that a mesh axis runs over, the one named last changes fastest.
Arguments:
- anomalies: float32 [65536, 2048], P('rows', 'cols'), may hold values from -75 to 75
- pairing: int32 [2, 16], replicated, may hold values from 0 to 15, as said below
Outputs:
- rotated: float32 [65536, 2048], P('rows', 'cols')
The draws below stay inside these ranges and needn't reach their ends.
Inputs may be any that keep to these rules, and one draw needn't show every extreme that they name: pairing[r, b] = b XOR m_r with one m_r for the whole row r; m_0 is neither 0 nor 2048 // 128 - 1, and for odd r m_r is m_0 with every bit of 15 flipped, for even r it is m_0.
All inputs are finite; a program needn't handle non-finite values.
Results may differ from the reference program's by a relative error of at most 0.0003.
Values sent between devices are 32-bit elements; how exact they have to be, the bound alone decides.
No kernel may reach another device: no remote copies, remote signals or barrier semaphores. Data moves between devices by JAX's collectives and lax.ppermute only.
A program may use at most 128 MiB of HBM per device.

```python
import math
import jax
import jax.numpy as jnp
from jax import lax

BLK = 128
SHIFTS = 8
ROUNDS = 2
SOUNDINGS = 65536
MEMBERS = 2048


def draw_anomalies(key, part):
    subkeys = jax.random.split(key, 5)
    position = (jnp.arange(SOUNDINGS, dtype=jnp.float32)[:, None] + 0.5) / SOUNDINGS
    rising = 1.0 + 2.0 * position
    roughness = jax.random.uniform(subkeys[0], (SOUNDINGS, 1), jnp.float32, 0.5, 1.5)
    column_scale = jnp.exp(jax.random.uniform(subkeys[1], (1, MEMBERS), jnp.float32, math.log(0.3), math.log(3.0)))
    row_factor = jnp.clip(jax.random.normal(subkeys[2], (SOUNDINGS, 1), jnp.float32), -5.0, 5.0)
    column_factor = jnp.clip(jax.random.normal(subkeys[3], (1, MEMBERS), jnp.float32), -5.0, 5.0)
    noise_field = jnp.clip(jax.random.normal(subkeys[4], (SOUNDINGS, MEMBERS), jnp.float32), -5.0, 5.0)
    strength = 0.2 + 0.8 * position
    values = 0.3 * rising * roughness * (noise_field * column_scale + strength * row_factor * column_factor)
    return values.astype(jnp.float32)


def draw_pairing(key, part):
    block_total = MEMBERS // BLK
    first_mask = jax.random.randint(key, (), 1, block_total - 1)
    all_bits = block_total - 1
    round_ids = jnp.arange(ROUNDS)
    round_masks = jnp.where(round_ids % 2 == 0, first_mask, jnp.bitwise_xor(first_mask, all_bits))
    indices = jnp.arange(block_total)
    return jnp.bitwise_xor(indices[None, :], round_masks[:, None]).astype(jnp.int32)


def setup_inputs(seed: int = 0) -> dict:
    arg_keys = jax.random.split(jax.random.key(seed), 3)
    return {
        "anomalies": draw_anomalies(jax.random.fold_in(arg_keys[2], 71), 0),
        "pairing": draw_pairing(jax.random.fold_in(arg_keys[2], 71), 0),
    }


TIE_GUARD = 1e-06

def block_product(left, right):
    return jnp.dot(left.T, right, precision=lax.Precision.HIGHEST, preferred_element_type=jnp.float32)

def apply_turn(data, coef):
    return jnp.dot(data, coef, precision=lax.Precision.HIGHEST, preferred_element_type=jnp.float32)

def rotate_pair(gram_ll, gram_lr, gram_rl, gram_rr, shifts):
    width = gram_ll.shape[0]
    eye_block = jnp.eye(width, dtype=jnp.float32)
    empty_block = jnp.zeros((width, width), jnp.float32)
    turn_ll, turn_lr, turn_rl, turn_rr = (eye_block, empty_block, empty_block, eye_block)
    for shift_step in range(shifts):
        if shift_step > 0:
            gram_lr = jnp.roll(gram_lr, -1, axis=1)
            gram_rl = jnp.roll(gram_rl, -1, axis=0)
            gram_rr = jnp.roll(jnp.roll(gram_rr, -1, axis=0), -1, axis=1)
            turn_lr = jnp.roll(turn_lr, -1, axis=1)
            turn_rr = jnp.roll(turn_rr, -1, axis=1)
        left_diag = jnp.diagonal(gram_ll)
        right_diag = jnp.diagonal(gram_rr)
        cross_diag = jnp.diagonal(gram_lr)
        gap_value = right_diag - left_diag
        gap_sign = jnp.where(gap_value >= 0.0, 1.0, -1.0).astype(gap_value.dtype)
        denom = jnp.abs(gap_value) + jnp.sqrt(gap_value * gap_value + 4.0 * cross_diag * cross_diag) + TIE_GUARD * (left_diag + right_diag)
        tangent = 2.0 * cross_diag * gap_sign / denom
        cosine = 1.0 / jnp.sqrt(1.0 + tangent * tangent)
        sine_value = cosine * tangent
        col_cos = cosine[None, :]
        col_sin = sine_value[None, :]
        upper_left = gram_ll * col_cos - gram_lr * col_sin
        upper_right = gram_ll * col_sin + gram_lr * col_cos
        lower_left = gram_rl * col_cos - gram_rr * col_sin
        lower_right = gram_rl * col_sin + gram_rr * col_cos
        row_cos = cosine[:, None]
        row_sin = sine_value[:, None]
        gram_ll = row_cos * upper_left - row_sin * lower_left
        gram_lr = row_cos * upper_right - row_sin * lower_right
        gram_rl = row_sin * upper_left + row_cos * lower_left
        gram_rr = row_sin * upper_right + row_cos * lower_right
        new_ll = turn_ll * col_cos - turn_lr * col_sin
        new_lr = turn_ll * col_sin + turn_lr * col_cos
        new_rl = turn_rl * col_cos - turn_rr * col_sin
        new_rr = turn_rl * col_sin + turn_rr * col_cos
        turn_ll, turn_lr, turn_rl, turn_rr = (new_ll, new_lr, new_rl, new_rr)
    back_steps = shifts - 1
    turn_lr = jnp.roll(turn_lr, back_steps, axis=1)
    turn_rr = jnp.roll(turn_rr, back_steps, axis=1)
    gram_rr = jnp.roll(jnp.roll(gram_rr, back_steps, axis=0), back_steps, axis=1)
    return ((turn_ll, turn_lr, turn_rl, turn_rr), (gram_ll, gram_rr))

def pair_output(current, pair_row, block_index):
    partner = pair_row[block_index].astype(jnp.int32)
    low_index = jnp.minimum(block_index, partner).astype(jnp.int32)
    high_index = jnp.maximum(block_index, partner).astype(jnp.int32)
    low_cols = lax.dynamic_slice_in_dim(current, (low_index * BLK).astype(jnp.int32), BLK, 1)
    high_cols = lax.dynamic_slice_in_dim(current, (high_index * BLK).astype(jnp.int32), BLK, 1)
    gram_ll = block_product(low_cols, low_cols)
    gram_lr = block_product(low_cols, high_cols)
    gram_rr = block_product(high_cols, high_cols)
    turns, grams = rotate_pair(gram_ll, gram_lr, gram_lr.T, gram_rr, SHIFTS)
    is_low = block_index == low_index
    coef_low = jnp.where(is_low, turns[0], turns[1])
    coef_high = jnp.where(is_low, turns[2], turns[3])
    return apply_turn(low_cols, coef_low) + apply_turn(high_cols, coef_high)

def reference(anomalies, pairing):
    block_total = MEMBERS // BLK
    current = anomalies
    for round_index in range(ROUNDS):
        pair_row = pairing[round_index]

        def one_block(block_index, current=current, pair_row=pair_row):
            return pair_output(current, pair_row, block_index)
        stacked = lax.map(one_block, jnp.arange(block_total, dtype=jnp.int32))
        current = jnp.transpose(stacked, (1, 0, 2)).reshape(SOUNDINGS, MEMBERS)
    return current
```

```python
from functools import partial

import jax
import jax.numpy as jnp
from jax import lax
from jax.experimental import pallas as pl
from jax.experimental.pallas import tpu as pltpu
from jax.sharding import PartitionSpec as P

BLK = 128
SHIFTS = 8
TIE_GUARD = 1e-06
COLS = 16
ROWS = 16
ALL_BITS = COLS - 1
CROSS = ((0, 1), (2, 3), (0, 2), (1, 3), (0, 3), (1, 2))
VMEM = pl.BlockSpec(memory_space=pltpu.VMEM)
SMEM = pl.BlockSpec(memory_space=pltpu.SMEM)
PARAMS = pltpu.CompilerParams(vmem_limit_bytes=40 * 1024 * 1024)


def route(mask):
    return [(b, b ^ mask) for b in range(COLS)]


def split(x):
    high = x.astype(jnp.bfloat16)
    return high, (x - high.astype(jnp.float32)).astype(jnp.bfloat16)


def tdot(left, right):
    return lax.dot_general(
        left, right, (((0,), (0,)), ((), ())), preferred_element_type=jnp.float32
    )


def dot(left, right):
    return jnp.dot(left, right, preferred_element_type=jnp.float32)


def dot3(left, right, product):
    lh, ll = split(left)
    rh, rl = split(right)
    return product(lh, rh) + (product(lh, rl) + product(ll, rh))


def gram_kernel(slots, x0, x1, x2, x3, cross, high, low):
    for index, x in enumerate((x0, x1, x2, x3)):
        h, l = split(x[...])
        high[slots[index]] = h
        low[slots[index]] = l
    for index, (a, b) in enumerate(CROSS):
        cross[index * BLK : (index + 1) * BLK, :] = tdot(high[a], high[b]) + (
            tdot(high[a], low[b]) + tdot(low[a], high[b])
        )


def gram_cross(slots, pieces):
    rows = pieces[0].shape[0]
    return pl.pallas_call(
        gram_kernel,
        out_shape=(
            jax.ShapeDtypeStruct((6 * BLK, BLK), jnp.float32),
            jax.ShapeDtypeStruct((4, rows, BLK), jnp.bfloat16),
            jax.ShapeDtypeStruct((4, rows, BLK), jnp.bfloat16),
        ),
        in_specs=[SMEM] + [VMEM] * 4,
        out_specs=(VMEM, VMEM, VMEM),
        compiler_params=PARAMS,
        name="gram_cross",
    )(slots, *pieces)


def turn_steps(gram, turn):
    row_id = lax.broadcasted_iota(jnp.int32, (BLK, BLK), 0)
    col_id = lax.broadcasted_iota(jnp.int32, (BLK, BLK), 1)
    eye = row_id == col_id
    for pair in range(2):
        unit = eye.astype(jnp.float32)
        zero = jnp.zeros((BLK, BLK), jnp.float32)
        for index, value in enumerate((unit, zero, zero, unit)):
            turn[pair, index] = value

    def diag(value):
        return jnp.sum(jnp.where(eye, value, 0.0), axis=0, keepdims=True)

    def upright(value):
        return jnp.sum(jnp.where(eye, value, 0.0), axis=1, keepdims=True)

    def back(value, axis):
        return pltpu.roll(value, BLK - 1, axis)

    def step(_, carry):
        for pair in range(2):
            ll, lr, rl, rr = (gram[pair, index] for index in range(4))
            a, g, e = diag(ll), diag(lr), diag(rr)
            gap = e - a
            sign = jnp.where(gap >= 0.0, 1.0, -1.0)
            denom = jnp.abs(gap) + jnp.sqrt(gap * gap + 4.0 * g * g) + TIE_GUARD * (a + e)
            tangent = 2.0 * g * sign / denom
            cosine = 1.0 / jnp.sqrt(1.0 + tangent * tangent)
            sine = cosine * tangent
            row_cos, row_sin = upright(cosine), upright(sine)
            ul = ll * cosine - lr * sine
            ur = ll * sine + lr * cosine
            dl = rl * cosine - rr * sine
            dr = rl * sine + rr * cosine
            gram[pair, 0] = row_cos * ul - row_sin * dl
            gram[pair, 1] = back(row_cos * ur - row_sin * dr, 1)
            gram[pair, 2] = back(row_sin * ul + row_cos * dl, 0)
            gram[pair, 3] = back(back(row_sin * ur + row_cos * dr, 0), 1)
            for side in (0, 2):
                left, right = turn[pair, side], turn[pair, side + 1]
                turn[pair, side] = left * cosine - right * sine
                turn[pair, side + 1] = back(left * sine + right * cosine, 1)
        return carry

    lax.fori_loop(0, SHIFTS, step, 0)
    for pair in range(2):
        for index in (1, 3):
            turn[pair, index] = pltpu.roll(turn[pair, index], SHIFTS, 1)
        gram[pair, 3] = pltpu.roll(pltpu.roll(gram[pair, 3], SHIFTS, 0), SHIFTS, 1)


def turn_kernel(places, cross, own, out_high, out_low, gram, turn, first):
    def block(index):
        return cross[index * BLK : (index + 1) * BLK, :]

    for pair in range(2):
        gram[pair, 0] = own[places[2 * pair]]
        gram[pair, 1] = block(pair)
        gram[pair, 2] = block(pair).T
        gram[pair, 3] = own[places[2 * pair + 1]]
    turn_steps(gram, turn)
    for pair in range(2):
        for side in range(2):
            first[pair, side, :BLK] = turn[pair, side]
            first[pair, side, BLK:] = turn[pair, 2 + side]
    both = jnp.concatenate(
        [
            jnp.concatenate([block(2), block(4)], axis=1),
            jnp.concatenate([block(5), block(3)], axis=1),
        ],
        axis=0,
    )
    left = [gram[0, 0], gram[0, 3]]
    right = [gram[1, 0], gram[1, 3]]
    for side in range(2):
        half = dot3(both, first[1, side], dot)
        mixed = dot3(first[0, side], half, tdot)
        gram[side, 0] = left[side]
        gram[side, 1] = mixed
        gram[side, 2] = mixed.T
        gram[side, 3] = right[side]
    turn_steps(gram, turn)
    for side in range(2):
        for pair in range(2):
            for late in range(2):
                value = dot3(first[pair, side], turn[side, 2 * pair + late], dot)
                h, l = split(value)
                out_high[2 * late + side, 2 * BLK * pair : 2 * BLK * (pair + 1), :] = h
                out_low[2 * late + side, 2 * BLK * pair : 2 * BLK * (pair + 1), :] = l


def turns(places, cross, own):
    return pl.pallas_call(
        turn_kernel,
        out_shape=(
            jax.ShapeDtypeStruct((4, 4 * BLK, BLK), jnp.bfloat16),
            jax.ShapeDtypeStruct((4, 4 * BLK, BLK), jnp.bfloat16),
        ),
        in_specs=[SMEM, VMEM, VMEM],
        out_specs=(VMEM, VMEM),
        scratch_shapes=[
            pltpu.VMEM((2, 4, BLK, BLK), jnp.float32),
            pltpu.VMEM((2, 4, BLK, BLK), jnp.float32),
            pltpu.VMEM((2, 2, 2 * BLK, BLK), jnp.float32),
        ],
        compiler_params=PARAMS,
        name="turns",
    )(places, cross, own)


def apply_kernel(slots, high, low, w_high, w_low, *outs):
    xh = jnp.concatenate([high[j] for j in range(4)], axis=1)
    xl = jnp.concatenate([low[j] for j in range(4)], axis=1)
    for index, out in enumerate(outs):
        wh, wl = w_high[slots[index]], w_low[slots[index]]
        out[...] = dot(xh, wh) + (dot(xh, wl) + dot(xl, wh))


def apply_turn(slots, high, low, w_high, w_low, count):
    rows = high.shape[1]
    return pl.pallas_call(
        apply_kernel,
        out_shape=tuple(jax.ShapeDtypeStruct((rows, BLK), jnp.float32) for _ in range(count)),
        in_specs=[SMEM] + [VMEM] * 4,
        out_specs=tuple([VMEM] * count),
        compiler_params=PARAMS,
        name="apply_turn",
    )(slots, high, low, w_high, w_low)


def to_all_rows(x):
    copies = jnp.broadcast_to(x, (ROWS, *x.shape))
    return lax.all_to_all(copies, "rows", split_axis=0, concat_axis=0, tiled=True)


def share_rows(x):
    parts = x.reshape(ROWS, x.shape[0] // ROWS, x.shape[1])
    return lax.all_to_all(parts, "rows", split_axis=0, concat_axis=0, tiled=True).sum(axis=0)


def group_plan(masks, block, slots):
    quarter = block.shape[0] // 4
    parts = block.reshape(4, quarter, BLK)
    piece = lambda j: lax.dynamic_index_in_dim(parts, slots[j], 0, keepdims=False)
    pieces = [piece(0)] + [lax.ppermute(piece(j + 1), "cols", route(m)) for j, m in enumerate(masks)]
    own = jnp.dot(
        block.T, block, precision=lax.Precision.HIGHEST, preferred_element_type=jnp.float32
    )
    own = share_rows(own)
    owns = jnp.stack([own] + [lax.ppermute(own, "cols", route(m)) for m in masks])
    owns = to_all_rows(owns)
    owns = jnp.transpose(owns, (1, 0, 2, 3)).reshape(4, BLK, BLK)
    cross, high, low = gram_cross(slots, pieces)
    cross = share_rows(cross)
    others = [lax.ppermute(cross, "cols", route(m)) for m in masks]
    cross = cross + others[0] + others[1] + others[2]
    cross = to_all_rows(cross).reshape(6 * BLK, BLK)
    places = jnp.zeros(4, jnp.int32).at[slots].set(jnp.arange(4, dtype=jnp.int32))
    w_high, w_low = turns(places, cross, owns)
    far = apply_turn(slots[1:], high, low, w_high, w_low, 3)
    back = [lax.ppermute(y, "cols", route(m)) for y, m in zip(far, masks)]
    (near,) = apply_turn(slots[:1], high, low, w_high, w_low, 1)
    out = parts
    for j, y in enumerate([near] + back):
        out = lax.dynamic_update_index_in_dim(out, y, slots[j], 0)
    return out.reshape(block.shape)


def on_device(anomalies, pairing):
    position = lax.axis_index("cols")
    mask = pairing[0, 0]
    late = mask ^ ALL_BITS
    first_bit = jnp.where(mask >= 8, 8, jnp.where(mask >= 4, 4, jnp.where(mask >= 2, 2, 1)))
    late_bit = jnp.where(late >= 8, 8, jnp.where(late >= 4, 4, jnp.where(late >= 2, 2, 1)))
    me = jnp.where(position & first_bit != 0, 1, 0) + jnp.where(position & late_bit != 0, 2, 0)
    small = jnp.minimum(mask, late)
    small_code = jnp.where(mask == small, 1, 2)
    slots = jnp.stack([me, me ^ small_code, me ^ (3 - small_code), me ^ 3]).astype(jnp.int32)
    branches = [partial(group_plan, (u, u ^ ALL_BITS, ALL_BITS)) for u in range(1, 8)]
    return lax.switch(small - 1, branches, anomalies, slots)


def solution(mesh):
    placed = (P("rows", "cols"), P())
    return jax.shard_map(
        on_device, mesh=mesh, in_specs=placed, out_specs=P("rows", "cols"), check_vma=False
    )
```

```python
from functools import partial

import jax
import jax.numpy as jnp
from jax import lax
from jax.experimental import pallas as pl
from jax.experimental.pallas import tpu as pltpu
from jax.sharding import PartitionSpec as P

BLK = 128
SHIFTS = 8
TIE_GUARD = 1e-06
COLS = 16
ROWS = 16
ALL_BITS = COLS - 1
STAY = 7
CROSS = ((0, 1), (2, 3), (0, 2), (1, 3), (0, 3), (1, 2))
VMEM = pl.BlockSpec(memory_space=pltpu.VMEM)
SMEM = pl.BlockSpec(memory_space=pltpu.SMEM)
ANY = pl.BlockSpec(memory_space=pl.ANY)
PARAMS = pltpu.CompilerParams(vmem_limit_bytes=40 * 1024 * 1024)


def route(mask):
    return [(b, b ^ mask) for b in range(COLS)]


def split(x):
    high = x.astype(jnp.bfloat16)
    return high, (x - high.astype(jnp.float32)).astype(jnp.bfloat16)


def tdot(left, right):
    return lax.dot_general(
        left, right, (((0,), (0,)), ((), ())), preferred_element_type=jnp.float32
    )


def dot(left, right):
    return jnp.dot(left, right, preferred_element_type=jnp.float32)


def dot3(left, right, product):
    lh, ll = split(left)
    rh, rl = split(right)
    return product(lh, rh) + (product(lh, rl) + product(ll, rh))


def odd(value):
    return bin(value).count("1") % 2


def halves(small):
    step = 2 if small == 1 else 1
    fits = [
        w
        for w in range(1, COLS)
        if not any(odd(w & m) for m in (small, ALL_BITS)) and odd(w & step)
    ]
    return fits[0]


def head_kernel(pairing, block, slots, p0, p1, p2, p3, e1, e2, e3, sems):
    position = lax.axis_index("cols")
    mask = pairing[0, 0]
    late = mask ^ ALL_BITS

    def top_bit(value):
        return jnp.where(value >= 8, 8, jnp.where(value >= 4, 4, jnp.where(value >= 2, 2, 1)))

    me = jnp.where((position & top_bit(mask)) != 0, 1, 0)
    me += jnp.where((position & top_bit(late)) != 0, 2, 0)
    small = jnp.minimum(mask, late)
    code = jnp.where(mask == small, 1, 2)
    places = (me, me ^ code, me ^ (3 - code), me ^ 3)
    rows = p0.shape[0]
    copies = []
    for index, (place, piece) in enumerate(zip(places, (p0, p1, p2, p3))):
        slots[index] = place
        source = block.at[pl.ds(pl.multiple_of(place * rows, rows), rows)]
        copies.append(pltpu.make_async_copy(source, piece, sems.at[index]))
        copies[-1].start()
    half = jnp.int32(halves(1))
    for u in range(2, 8):
        half = jnp.where(small == u, halves(u), half)
    half = half & position
    half = half ^ (half >> 2)
    half = (half ^ (half >> 1)) & 1
    slots[4] = small - 1
    slots[5] = jnp.where(half == 0, small - 1, STAY)
    slots[6] = jnp.where(half == 1, small - 1, STAY)
    slots[7] = small - 1
    for empty in (e1, e2, e3):
        empty[:8] = jnp.zeros((8, BLK), jnp.float32)
    for copy in copies:
        copy.wait()


def head(pairing, block):
    quarter = jax.ShapeDtypeStruct((block.shape[0] // 4, BLK), jnp.float32)
    return pl.pallas_call(
        head_kernel,
        out_shape=(jax.ShapeDtypeStruct((8,), jnp.int32),) + (quarter,) * 7,
        in_specs=[SMEM, ANY],
        out_specs=(SMEM,) + (VMEM,) * 7,
        scratch_shapes=[pltpu.SemaphoreType.DMA((4,))],
        compiler_params=PARAMS,
        name="head",
    )(pairing, block)


def tail_kernel(slots, y0, y1, y2, y3, out, sems):
    rows = y0.shape[0]
    copies = []
    for index, y in enumerate((y0, y1, y2, y3)):
        target = out.at[pl.ds(pl.multiple_of(slots[index] * rows, rows), rows)]
        copies.append(pltpu.make_async_copy(y, target, sems.at[index]))
        copies[-1].start()
    for copy in copies:
        copy.wait()


def tail(slots, pieces):
    rows = pieces[0].shape[0]
    return pl.pallas_call(
        tail_kernel,
        out_shape=jax.ShapeDtypeStruct((4 * rows, BLK), jnp.float32),
        in_specs=[SMEM] + [VMEM] * 4,
        out_specs=ANY,
        scratch_shapes=[pltpu.SemaphoreType.DMA((4,))],
        compiler_params=PARAMS,
        name="tail",
    )(slots, *pieces)


def gram_kernel(slots, own, x0, x1, x2, x3, part, high, low):
    for index, x in enumerate((x0, x1, x2, x3)):
        h, l = split(x[...])
        high[slots[index]] = h
        low[slots[index]] = l
    for index, (a, b) in enumerate(CROSS):
        value = tdot(high[a], high[b]) + (tdot(high[a], low[b]) + tdot(low[a], high[b]))
        part[:, index] = value.reshape(ROWS, BLK // ROWS, BLK)
    part[:, len(CROSS)] = own[...].reshape(ROWS, BLK // ROWS, BLK)


def gram_cross(slots, own, pieces):
    rows = pieces[0].shape[0]
    return pl.pallas_call(
        gram_kernel,
        out_shape=(
            jax.ShapeDtypeStruct((ROWS, len(CROSS) + 1, BLK // ROWS, BLK), jnp.float32),
            jax.ShapeDtypeStruct((4, rows, BLK), jnp.bfloat16),
            jax.ShapeDtypeStruct((4, rows, BLK), jnp.bfloat16),
        ),
        in_specs=[SMEM] + [VMEM] * 5,
        out_specs=(VMEM, VMEM, VMEM),
        compiler_params=PARAMS,
        name="gram_cross",
    )(slots, own, *pieces)


def spread_kernel(a, b, c, d, out):
    count = len(CROSS)
    cross = (a[:count] + b[:count]) + (c[:count] + d[:count])
    whole = jnp.concatenate([cross] + [x[count:] for x in (a, b, c, d)])
    out[...] = jnp.broadcast_to(whole, out.shape)


def spread(parts):
    return pl.pallas_call(
        spread_kernel,
        out_shape=jax.ShapeDtypeStruct((ROWS, len(CROSS) + 4, BLK // ROWS, BLK), jnp.float32),
        in_specs=[VMEM] * 4,
        out_specs=VMEM,
        compiler_params=PARAMS,
        name="spread",
    )(*parts)


def turn_steps(gram, turn):
    row_id = lax.broadcasted_iota(jnp.int32, (BLK, BLK), 0)
    col_id = lax.broadcasted_iota(jnp.int32, (BLK, BLK), 1)
    eye = row_id == col_id
    for pair in range(2):
        unit = eye.astype(jnp.float32)
        zero = jnp.zeros((BLK, BLK), jnp.float32)
        for index, value in enumerate((unit, zero, zero, unit)):
            turn[pair, index] = value

    def diag(value):
        return jnp.sum(jnp.where(eye, value, 0.0), axis=0, keepdims=True)

    def upright(value):
        return jnp.sum(jnp.where(eye, value, 0.0), axis=1, keepdims=True)

    def back(value, axis):
        return pltpu.roll(value, BLK - 1, axis)

    def step(_, carry):
        for pair in range(2):
            ll, lr, rl, rr = (gram[pair, index] for index in range(4))
            a, g, e = diag(ll), diag(lr), diag(rr)
            gap = e - a
            sign = jnp.where(gap >= 0.0, 1.0, -1.0)
            denom = jnp.abs(gap) + jnp.sqrt(gap * gap + 4.0 * g * g) + TIE_GUARD * (a + e)
            tangent = 2.0 * g * sign / denom
            cosine = 1.0 / jnp.sqrt(1.0 + tangent * tangent)
            sine = cosine * tangent
            row_cos, row_sin = upright(cosine), upright(sine)
            ul = ll * cosine - lr * sine
            ur = ll * sine + lr * cosine
            dl = rl * cosine - rr * sine
            dr = rl * sine + rr * cosine
            gram[pair, 0] = row_cos * ul - row_sin * dl
            gram[pair, 1] = back(row_cos * ur - row_sin * dr, 1)
            gram[pair, 2] = back(row_sin * ul + row_cos * dl, 0)
            gram[pair, 3] = back(back(row_sin * ur + row_cos * dr, 0), 1)
            for side in (0, 2):
                left, right = turn[pair, side], turn[pair, side + 1]
                turn[pair, side] = left * cosine - right * sine
                turn[pair, side + 1] = back(left * sine + right * cosine, 1)
        return carry

    lax.fori_loop(0, SHIFTS, step, 0)
    for pair in range(2):
        for index in (1, 3):
            turn[pair, index] = pltpu.roll(turn[pair, index], SHIFTS, 1)
        gram[pair, 3] = pltpu.roll(pltpu.roll(gram[pair, 3], SHIFTS, 0), SHIFTS, 1)


def turn_kernel(slots, sums, out_high, out_low, gram, turn, first):
    def place(which):
        found = jnp.int32(0)
        for j in range(1, 4):
            found = jnp.where(slots[j] == which, j, found)
        return found

    def block(index):
        return sums[:, index].reshape(BLK, BLK)

    for pair in range(2):
        gram[pair, 0] = block(len(CROSS) + place(2 * pair))
        gram[pair, 1] = block(pair)
        gram[pair, 2] = block(pair).T
        gram[pair, 3] = block(len(CROSS) + place(2 * pair + 1))
    turn_steps(gram, turn)
    for pair in range(2):
        for side in range(2):
            first[pair, side, :BLK] = turn[pair, side]
            first[pair, side, BLK:] = turn[pair, 2 + side]
    both = jnp.concatenate(
        [
            jnp.concatenate([block(2), block(4)], axis=1),
            jnp.concatenate([block(5), block(3)], axis=1),
        ],
        axis=0,
    )
    left = [gram[0, 0], gram[0, 3]]
    right = [gram[1, 0], gram[1, 3]]
    for side in range(2):
        half = dot3(both, first[1, side], dot)
        mixed = dot3(first[0, side], half, tdot)
        gram[side, 0] = left[side]
        gram[side, 1] = mixed
        gram[side, 2] = mixed.T
        gram[side, 3] = right[side]
    turn_steps(gram, turn)
    for side in range(2):
        for pair in range(2):
            for late in range(2):
                value = dot3(first[pair, side], turn[side, 2 * pair + late], dot)
                h, l = split(value)
                out_high[2 * late + side, 2 * BLK * pair : 2 * BLK * (pair + 1), :] = h
                out_low[2 * late + side, 2 * BLK * pair : 2 * BLK * (pair + 1), :] = l


def turns(slots, sums):
    return pl.pallas_call(
        turn_kernel,
        out_shape=(
            jax.ShapeDtypeStruct((4, 4 * BLK, BLK), jnp.bfloat16),
            jax.ShapeDtypeStruct((4, 4 * BLK, BLK), jnp.bfloat16),
        ),
        in_specs=[SMEM, VMEM],
        out_specs=(VMEM, VMEM),
        scratch_shapes=[
            pltpu.VMEM((2, 4, BLK, BLK), jnp.float32),
            pltpu.VMEM((2, 4, BLK, BLK), jnp.float32),
            pltpu.VMEM((2, 2, 2 * BLK, BLK), jnp.float32),
        ],
        compiler_params=PARAMS,
        name="turns",
    )(slots, sums)


def apply_kernel(which, slots, high, low, w_high, w_low, *outs):
    step = 256

    def body(index, carry):
        rows = pl.ds(index * step, step)
        xh = jnp.concatenate([high[j, rows] for j in range(4)], axis=1)
        xl = jnp.concatenate([low[j, rows] for j in range(4)], axis=1)
        for j, out in zip(which, outs):
            wh, wl = w_high[slots[j]], w_low[slots[j]]
            out[rows, :] = dot(xh, wh) + (dot(xh, wl) + dot(xl, wh))
        return carry

    lax.fori_loop(0, high.shape[1] // step, body, 0)


def apply_turn(slots, which, high, low, w_high, w_low):
    piece = jax.ShapeDtypeStruct(high.shape[1:], jnp.float32)
    return pl.pallas_call(
        partial(apply_kernel, which),
        out_shape=[piece] * len(which),
        in_specs=[SMEM] + [VMEM] * 4,
        out_specs=[VMEM] * len(which),
        compiler_params=PARAMS,
        name="apply_turn",
    )(slots, high, low, w_high, w_low)


def own_kernel(p0, p1, p2, p3, out):
    def product(x):
        h, l = split(x)
        return tdot(h, h) + (tdot(h, l) + tdot(l, h))

    step = 256
    out[...] = jnp.zeros((BLK, BLK), jnp.float32)

    def body(index, carry):
        total = out[...]
        for p in (p0, p1, p2, p3):
            total += product(p[pl.ds(index * step, step), :])
        out[...] = total
        return carry

    lax.fori_loop(0, p0.shape[0] // step, body, 0)


def own_gram(pieces):
    return pl.pallas_call(
        own_kernel,
        out_shape=jax.ShapeDtypeStruct((BLK, BLK), jnp.float32),
        in_specs=[VMEM] * 4,
        out_specs=VMEM,
        compiler_params=PARAMS,
        name="own_gram",
    )(*pieces)


def swap(masks, parts):
    return [lax.ppermute(x, "cols", route(m)) for x, m in zip(parts, masks)]


def gate_kernel(token, p1, p2, p3, q1, q2, q3):
    pass


def gate(token, pieces):
    return pl.pallas_call(
        gate_kernel,
        out_shape=[jax.ShapeDtypeStruct(p.shape, p.dtype) for p in pieces],
        in_specs=[VMEM] + [ANY] * 3,
        out_specs=[ANY] * 3,
        input_output_aliases={1: 0, 2: 1, 3: 2},
        compiler_params=PARAMS,
        name="gate",
    )(token, *pieces)


def bring(masks, parts, came):
    return swap(masks, parts)


def leave(parts, came):
    return list(came)


def share(masks, part):
    return swap(masks, [part] * 3)


def by_mask(which, function, *operands, other=None):
    branches = [partial(function, (u, u ^ ALL_BITS, ALL_BITS)) for u in range(1, 8)]
    if other is not None:
        branches.append(other)
    return lax.switch(which, branches, *operands)


def over_rows(x):
    return lax.all_to_all(x, "rows", split_axis=0, concat_axis=0, tiled=True)


def on_device(anomalies, pairing):
    slots, first, *rest = head(pairing, anomalies)
    which = slots[4]

    def stay(parts, came, near, own):
        return list(parts), near, own

    def hand_on(parts, came, near, own):
        token = came[0][:8] + came[1][:8] + came[2][:8]
        token = lax.ppermute(token, "cols", route(1)) + lax.ppermute(token, "cols", route(2))
        own = own_gram([near, *parts])
        return list(gate(token, parts)), near, own

    def middle(parts, came, near, own):
        part, high, low = gram_cross(slots, own, [near, *came])
        part = over_rows(part).sum(axis=0)
        sums = over_rows(spread([part] + by_mask(which, share, part)))
        w_high, w_low = turns(slots, sums)
        near, *far = apply_turn(slots, (0, 1, 2, 3), high, low, w_high, w_low)
        return far, near, own

    def wave(number, carry):
        parts, came, near, own = carry
        parts, near, own = lax.switch(number, [stay, hand_on, middle], parts, came, near, own)
        now = lax.dynamic_index_in_dim(slots, 5 + number, 0, keepdims=False)
        return parts, by_mask(now, bring, parts, came, other=leave), near, own

    own = jnp.zeros((BLK, BLK), jnp.float32)
    _, came, near, _ = lax.fori_loop(0, 3, wave, (rest[:3], rest[3:], first, own))
    return tail(slots, [near, *came])


def solution(mesh):
    placed = (P("rows", "cols"), P())
    return jax.shard_map(
        on_device, mesh=mesh, in_specs=placed, out_specs=P("rows", "cols"), check_vma=False
    )
```

```python
from functools import partial

import jax
import jax.numpy as jnp
from jax import lax
from jax.experimental import pallas as pl
from jax.experimental.pallas import tpu as pltpu
from jax.sharding import PartitionSpec as P

BLK = 128
SHIFTS = 8
TIE_GUARD = 1e-06
COLS = 16
ROWS = 16
ALL_BITS = COLS - 1
STAY = 7
CROSS = ((0, 1), (2, 3), (0, 2), (1, 3), (0, 3), (1, 2))
VMEM = pl.BlockSpec(memory_space=pltpu.VMEM)
SMEM = pl.BlockSpec(memory_space=pltpu.SMEM)
ANY = pl.BlockSpec(memory_space=pl.ANY)
PARAMS = pltpu.CompilerParams(vmem_limit_bytes=40 * 1024 * 1024)


def route(mask):
    return [(b, b ^ mask) for b in range(COLS)]


def split(x):
    high = x.astype(jnp.bfloat16)
    return high, (x - high.astype(jnp.float32)).astype(jnp.bfloat16)


def tdot(left, right):
    return lax.dot_general(
        left, right, (((0,), (0,)), ((), ())), preferred_element_type=jnp.float32
    )


def dot(left, right):
    return jnp.dot(left, right, preferred_element_type=jnp.float32)


def dot3(left, right, product):
    lh, ll = split(left)
    rh, rl = split(right)
    return product(lh, rh) + (product(lh, rl) + product(ll, rh))


def odd(value):
    return bin(value).count("1") % 2


def halves(small):
    step = 2 if small == 1 else 1
    fits = [
        w
        for w in range(1, COLS)
        if not any(odd(w & m) for m in (small, ALL_BITS)) and odd(w & step)
    ]
    return fits[0]


def head_kernel(pairing, block, slots, p0, p1, p2, p3, e1, e2, e3, sems):
    position = lax.axis_index("cols")
    mask = pairing[0, 0]
    late = mask ^ ALL_BITS

    def top_bit(value):
        return jnp.where(value >= 8, 8, jnp.where(value >= 4, 4, jnp.where(value >= 2, 2, 1)))

    me = jnp.where((position & top_bit(mask)) != 0, 1, 0)
    me += jnp.where((position & top_bit(late)) != 0, 2, 0)
    small = jnp.minimum(mask, late)
    code = jnp.where(mask == small, 1, 2)
    places = (me, me ^ code, me ^ (3 - code), me ^ 3)
    rows = p0.shape[0]
    copies = []
    for index, (place, piece) in enumerate(zip(places, (p0, p1, p2, p3))):
        slots[index] = place
        source = block.at[pl.ds(pl.multiple_of(place * rows, rows), rows)]
        copies.append(pltpu.make_async_copy(source, piece, sems.at[index]))
        copies[-1].start()
    half = jnp.int32(halves(1))
    for u in range(2, 8):
        half = jnp.where(small == u, halves(u), half)
    half = half & position
    half = half ^ (half >> 2)
    half = (half ^ (half >> 1)) & 1
    slots[4] = small - 1
    slots[5] = jnp.where(half == 0, small - 1, STAY)
    slots[6] = jnp.where(half == 1, small - 1, STAY)
    slots[7] = small - 1
    slots[8] = 0
    slots[9] = jnp.where(small == 1, 2, 1)
    slots[10] = 3
    slots[11] = 0
    for empty in (e1, e2, e3):
        empty[:8] = jnp.zeros((8, BLK), jnp.float32)
    for copy in copies:
        copy.wait()


def head(pairing, block):
    quarter = jax.ShapeDtypeStruct((block.shape[0] // 4, BLK), jnp.float32)
    return pl.pallas_call(
        head_kernel,
        out_shape=(jax.ShapeDtypeStruct((12,), jnp.int32),) + (quarter,) * 7,
        in_specs=[SMEM, pl.BlockSpec(memory_space=pltpu.HBM)],
        out_specs=(SMEM,) + (VMEM,) * 7,
        scratch_shapes=[pltpu.SemaphoreType.DMA((4,))],
        compiler_params=PARAMS,
        name="head",
    )(pairing, block)


def tail_kernel(slots, y0, y1, y2, y3, out, sems):
    rows = y0.shape[0]
    copies = []
    for index, y in enumerate((y0, y1, y2, y3)):
        target = out.at[pl.ds(pl.multiple_of(slots[index] * rows, rows), rows)]
        copies.append(pltpu.make_async_copy(y, target, sems.at[index]))
        copies[-1].start()
    for copy in copies:
        copy.wait()


def tail(slots, pieces):
    rows = pieces[0].shape[0]
    return pl.pallas_call(
        tail_kernel,
        out_shape=jax.ShapeDtypeStruct((4 * rows, BLK), jnp.float32),
        in_specs=[SMEM] + [VMEM] * 4,
        out_specs=ANY,
        scratch_shapes=[pltpu.SemaphoreType.DMA((4,))],
        compiler_params=PARAMS,
        name="tail",
    )(slots, *pieces)


def gram_kernel(slots, own, x0, x1, x2, x3, part, high, low):
    for index, x in enumerate((x0, x1, x2, x3)):
        h, l = split(x[...])
        high[slots[index]] = h
        low[slots[index]] = l
    def keep(index, value):
        part[:, index] = value.reshape(ROWS, BLK // ROWS, BLK)

    def wide(x, a):
        return jnp.concatenate([x[a], x[a + 1]], axis=1)

    for index, (a, b) in enumerate(CROSS[:2]):
        keep(index, tdot(high[a], high[b]) + (tdot(high[a], low[b]) + tdot(low[a], high[b])))
    value = tdot(wide(high, 0), wide(high, 2)) + (
        tdot(wide(high, 0), wide(low, 2)) + tdot(wide(low, 0), wide(high, 2))
    )
    for index, (a, b) in enumerate(CROSS[2:]):
        b = b - 2
        keep(2 + index, value[a * BLK : (a + 1) * BLK, b * BLK : (b + 1) * BLK])
    part[:, len(CROSS)] = own[...].reshape(ROWS, BLK // ROWS, BLK)


def gram_cross(slots, own, pieces):
    rows = pieces[0].shape[0]
    return pl.pallas_call(
        gram_kernel,
        out_shape=(
            jax.ShapeDtypeStruct((ROWS, len(CROSS) + 1, BLK // ROWS, BLK), jnp.float32),
            jax.ShapeDtypeStruct((4, rows, BLK), jnp.bfloat16),
            jax.ShapeDtypeStruct((4, rows, BLK), jnp.bfloat16),
        ),
        in_specs=[SMEM] + [VMEM] * 5,
        out_specs=(VMEM, VMEM, VMEM),
        compiler_params=PARAMS,
        name="gram_cross",
    )(slots, own, *pieces)


def spread_kernel(a, b, c, d, out):
    count = len(CROSS)
    cross = (a[:count] + b[:count]) + (c[:count] + d[:count])
    whole = jnp.concatenate([cross] + [x[count:] for x in (a, b, c, d)])
    out[...] = jnp.broadcast_to(whole, out.shape)


def spread(parts):
    return pl.pallas_call(
        spread_kernel,
        out_shape=jax.ShapeDtypeStruct((ROWS, len(CROSS) + 4, BLK // ROWS, BLK), jnp.float32),
        in_specs=[VMEM] * 4,
        out_specs=VMEM,
        compiler_params=PARAMS,
        name="spread",
    )(*parts)


def turn_steps(gram, turn):
    row_id = lax.broadcasted_iota(jnp.int32, (BLK, BLK), 0)
    col_id = lax.broadcasted_iota(jnp.int32, (BLK, BLK), 1)
    eye = row_id == col_id
    for pair in range(2):
        unit = eye.astype(jnp.float32)
        zero = jnp.zeros((BLK, BLK), jnp.float32)
        for index, value in enumerate((unit, zero, zero, unit)):
            turn[pair, index] = value

    def diag(value):
        return jnp.sum(jnp.where(eye, value, 0.0), axis=0, keepdims=True)

    def upright(value):
        return jnp.sum(jnp.where(eye, value, 0.0), axis=1, keepdims=True)

    def back(value, axis):
        return pltpu.roll(value, BLK - 1, axis)

    def angles(ll, lr, rl, rr):
        a, g, e = diag(ll), diag(lr), diag(rr)
        gap = e - a
        sign = jnp.where(gap >= 0.0, 1.0, -1.0)
        denom = jnp.abs(gap) + jnp.sqrt(gap * gap + 4.0 * g * g) + TIE_GUARD * (a + e)
        tangent = 2.0 * g * sign / denom
        cosine = 1.0 / jnp.sqrt(1.0 + tangent * tangent)
        return cosine, cosine * tangent

    def step(_, carry):
        grams = [[gram[pair, index] for index in range(4)] for pair in range(2)]
        rows = [angles(*blocks) for blocks in grams]
        upper = [
            (ll * c - lr * s, ll * s + lr * c, rl * c - rr * s, rl * s + rr * c)
            for (ll, lr, rl, rr), (c, s) in zip(grams, rows)
        ]
        columns = [(upright(c), upright(s)) for c, s in rows]
        for pair in range(2):
            c, s = rows[pair]
            for side in (0, 2):
                left, right = turn[pair, side], turn[pair, side + 1]
                turn[pair, side] = left * c - right * s
                turn[pair, side + 1] = back(left * s + right * c, 1)
        for pair in range(2):
            (ul, ur, dl, dr), (c, s) = upper[pair], columns[pair]
            gram[pair, 0] = c * ul - s * dl
            gram[pair, 1] = back(c * ur - s * dr, 1)
            gram[pair, 2] = back(s * ul + c * dl, 0)
            gram[pair, 3] = back(back(s * ur + c * dr, 0), 1)
        return carry

    lax.fori_loop(0, SHIFTS, step, 0)
    for pair in range(2):
        for index in (1, 3):
            turn[pair, index] = pltpu.roll(turn[pair, index], SHIFTS, 1)
        gram[pair, 3] = pltpu.roll(pltpu.roll(gram[pair, 3], SHIFTS, 0), SHIFTS, 1)


def turn_kernel(slots, sums, out_high, out_low, gram, turn, first):
    def place(which):
        found = jnp.int32(0)
        for j in range(1, 4):
            found = jnp.where(slots[j] == which, j, found)
        return found

    def block(index):
        return sums[:, index].reshape(BLK, BLK)

    for pair in range(2):
        gram[pair, 0] = block(len(CROSS) + place(2 * pair))
        gram[pair, 1] = block(pair)
        gram[pair, 2] = block(pair).T
        gram[pair, 3] = block(len(CROSS) + place(2 * pair + 1))
    turn_steps(gram, turn)
    for pair in range(2):
        for side in range(2):
            first[pair, side, :BLK] = turn[pair, side]
            first[pair, side, BLK:] = turn[pair, 2 + side]
    both = jnp.concatenate(
        [
            jnp.concatenate([block(2), block(4)], axis=1),
            jnp.concatenate([block(5), block(3)], axis=1),
        ],
        axis=0,
    )
    left = [gram[0, 0], gram[0, 3]]
    right = [gram[1, 0], gram[1, 3]]
    for side in range(2):
        half = dot3(both, first[1, side], dot)
        mixed = dot3(first[0, side], half, tdot)
        gram[side, 0] = left[side]
        gram[side, 1] = mixed
        gram[side, 2] = mixed.T
        gram[side, 3] = right[side]
    turn_steps(gram, turn)
    for side in range(2):
        for pair in range(2):
            for late in range(2):
                value = dot3(first[pair, side], turn[side, 2 * pair + late], dot)
                h, l = split(value)
                out_high[2 * late + side, 2 * BLK * pair : 2 * BLK * (pair + 1), :] = h
                out_low[2 * late + side, 2 * BLK * pair : 2 * BLK * (pair + 1), :] = l


def turns(slots, sums):
    return pl.pallas_call(
        turn_kernel,
        out_shape=(
            jax.ShapeDtypeStruct((4, 4 * BLK, BLK), jnp.bfloat16),
            jax.ShapeDtypeStruct((4, 4 * BLK, BLK), jnp.bfloat16),
        ),
        in_specs=[SMEM, VMEM],
        out_specs=(VMEM, VMEM),
        scratch_shapes=[
            pltpu.VMEM((2, 4, BLK, BLK), jnp.float32),
            pltpu.VMEM((2, 4, BLK, BLK), jnp.float32),
            pltpu.VMEM((2, 2, 2 * BLK, BLK), jnp.float32),
        ],
        compiler_params=PARAMS,
        name="turns",
    )(slots, sums)


def apply_kernel(which, slots, high, low, w_high, w_low, *outs):
    step = 256

    def body(index, carry):
        rows = pl.ds(index * step, step)
        xh = jnp.concatenate([high[j, rows] for j in range(4)], axis=1)
        xl = jnp.concatenate([low[j, rows] for j in range(4)], axis=1)
        for j in range(0, len(which), 2):
            places = [slots[which[j]], slots[which[j + 1]]]
            wh = jnp.concatenate([w_high[p] for p in places], axis=1)
            wl = jnp.concatenate([w_low[p] for p in places], axis=1)
            value = dot(xh, wh) + (dot(xh, wl) + dot(xl, wh))
            outs[j][rows, :] = value[:, :BLK]
            outs[j + 1][rows, :] = value[:, BLK:]
        return carry

    lax.fori_loop(0, high.shape[1] // step, body, 0)


def apply_turn(slots, which, high, low, w_high, w_low):
    piece = jax.ShapeDtypeStruct(high.shape[1:], jnp.float32)
    return pl.pallas_call(
        partial(apply_kernel, which),
        out_shape=[piece] * len(which),
        in_specs=[SMEM] + [VMEM] * 4,
        out_specs=[VMEM] * len(which),
        compiler_params=PARAMS,
        name="apply_turn",
    )(slots, high, low, w_high, w_low)


def own_kernel(p0, p1, p2, p3, out):
    def product(x):
        h, l = split(x)
        return tdot(h, h) + (tdot(h, l) + tdot(l, h))

    step = 256
    out[...] = jnp.zeros((BLK, BLK), jnp.float32)

    def body(index, carry):
        total = out[...]
        for p in (p0, p1, p2, p3):
            total += product(p[pl.ds(index * step, step), :])
        out[...] = total
        return carry

    lax.fori_loop(0, p0.shape[0] // step, body, 0)


def own_gram(pieces):
    return pl.pallas_call(
        own_kernel,
        out_shape=jax.ShapeDtypeStruct((BLK, BLK), jnp.float32),
        in_specs=[VMEM] * 4,
        out_specs=VMEM,
        compiler_params=PARAMS,
        name="own_gram",
    )(*pieces)


def swap(masks, parts):
    return [lax.ppermute(x, "cols", route(m)) for x, m in zip(parts, masks)]


def gate_kernel(token, p1, p2, p3, q1, q2, q3):
    pass


def gate(token, pieces):
    return pl.pallas_call(
        gate_kernel,
        out_shape=[jax.ShapeDtypeStruct(p.shape, p.dtype) for p in pieces],
        in_specs=[VMEM] + [ANY] * 3,
        out_specs=[ANY] * 3,
        input_output_aliases={1: 0, 2: 1, 3: 2},
        compiler_params=PARAMS,
        name="gate",
    )(token, *pieces)


def bring(masks, parts, came, near, own):
    return swap(masks, parts), own


def leave(parts, came, near, own):
    return list(came), own_gram([near, *parts])


def share(masks, part):
    return swap(masks, [part] * 3)


def by_mask(which, function, *operands, other=None):
    branches = [partial(function, (u, u ^ ALL_BITS, ALL_BITS)) for u in range(1, 8)]
    if other is not None:
        branches.append(other)
    return lax.switch(which, branches, *operands)


def over_rows(x):
    return lax.all_to_all(x, "rows", split_axis=0, concat_axis=0, tiled=True)


def on_device(anomalies, pairing):
    slots, first, *rest = head(pairing, anomalies)
    which = slots[4]

    def stay(parts, came, near, own):
        return list(parts), near

    def hand_on(step, parts, came, near, own):
        token = came[0][:8] + came[1][:8] + came[2][:8]
        token = lax.ppermute(token, "cols", route(step))
        return list(gate(token, parts)), near

    def middle(parts, came, near, own):
        part, high, low = gram_cross(slots, own, [near, *came])
        part = over_rows(part).sum(axis=0)
        sums = over_rows(spread([part] + by_mask(which, share, part)))
        w_high, w_low = turns(slots, sums)
        near, *far = apply_turn(slots, (0, 1, 2, 3), high, low, w_high, w_low)
        return far, near

    def wave(number, carry):
        parts, came, near, own = carry
        stage = lax.dynamic_index_in_dim(slots, 8 + number, 0, keepdims=False)
        now = lax.dynamic_index_in_dim(slots, 5 + number, 0, keepdims=False)
        stages_of = [stay, partial(hand_on, 1), partial(hand_on, 2), middle]
        parts, near = lax.switch(stage, stages_of, parts, came, near, own)
        came, own = by_mask(now, bring, parts, came, near, own, other=leave)
        return parts, came, near, own

    own = jnp.zeros((BLK, BLK), jnp.float32)
    _, came, near, _ = lax.fori_loop(0, 3, wave, (rest[:3], rest[3:], first, own))
    return tail(slots, [near, *came])


def solution(mesh):
    placed = (P("rows", "cols"), P())
    return jax.shard_map(
        on_device, mesh=mesh, in_specs=placed, out_specs=P("rows", "cols"), check_vma=False
    )
```

```python
from functools import partial

import jax
import jax.numpy as jnp
from jax import lax
from jax.experimental import pallas as pl
from jax.experimental.pallas import tpu as pltpu
from jax.sharding import PartitionSpec as P

BLK = 128
SHIFTS = 8
TIE_GUARD = 1e-06
COLS = 16
ROWS = 16
ALL_BITS = COLS - 1
STAY = 7
CROSS = ((0, 1), (2, 3), (0, 2), (1, 3), (0, 3), (1, 2))
VMEM = pl.BlockSpec(memory_space=pltpu.VMEM)
SMEM = pl.BlockSpec(memory_space=pltpu.SMEM)
ANY = pl.BlockSpec(memory_space=pl.ANY)
PARAMS = pltpu.CompilerParams(vmem_limit_bytes=40 * 1024 * 1024)


def route(mask):
    return [(b, b ^ mask) for b in range(COLS)]


def split(x):
    high = x.astype(jnp.bfloat16)
    return high, (x - high.astype(jnp.float32)).astype(jnp.bfloat16)


def tdot(left, right):
    return lax.dot_general(
        left, right, (((0,), (0,)), ((), ())), preferred_element_type=jnp.float32
    )


def dot(left, right):
    return jnp.dot(left, right, preferred_element_type=jnp.float32)


def dot3(left, right, product):
    lh, ll = split(left)
    rh, rl = split(right)
    return product(lh, rh) + (product(lh, rl) + product(ll, rh))


def odd(value):
    return bin(value).count("1") % 2


def halves(small):
    step = 2 if small == 1 else 1
    fits = [
        w
        for w in range(1, COLS)
        if not any(odd(w & m) for m in (small, ALL_BITS)) and odd(w & step)
    ]
    return fits[0]


def head_kernel(pairing, block, slots, p0, p1, p2, p3, e1, e2, e3, sems):
    position = lax.axis_index("cols")
    mask = pairing[0, 0]
    late = mask ^ ALL_BITS

    def top_bit(value):
        return jnp.where(value >= 8, 8, jnp.where(value >= 4, 4, jnp.where(value >= 2, 2, 1)))

    me = jnp.where((position & top_bit(mask)) != 0, 1, 0)
    me += jnp.where((position & top_bit(late)) != 0, 2, 0)
    small = jnp.minimum(mask, late)
    code = jnp.where(mask == small, 1, 2)
    places = (me, me ^ code, me ^ (3 - code), me ^ 3)
    rows = p0.shape[0]
    copies = []
    for index, (place, piece) in enumerate(zip(places, (p0, p1, p2, p3))):
        slots[index] = place
        source = block.at[pl.ds(pl.multiple_of(place * rows, rows), rows)]
        copies.append(pltpu.make_async_copy(source, piece, sems.at[index]))
        copies[-1].start()
    half = jnp.int32(halves(1))
    for u in range(2, 8):
        half = jnp.where(small == u, halves(u), half)
    half = half & position
    half = half ^ (half >> 2)
    half = (half ^ (half >> 1)) & 1
    slots[4] = small - 1
    slots[5] = jnp.where(half == 0, small - 1, STAY)
    slots[6] = jnp.where(half == 1, small - 1, STAY) + 8 * jnp.where(small == 1, 2, 1)
    slots[7] = small - 1 + 8 * 3
    for empty in (e1, e2, e3):
        empty[:8] = jnp.zeros((8, BLK), jnp.float32)
    for copy in copies:
        copy.wait()


def head(pairing, block):
    quarter = jax.ShapeDtypeStruct((block.shape[0] // 4, BLK), jnp.float32)
    return pl.pallas_call(
        head_kernel,
        out_shape=(jax.ShapeDtypeStruct((8,), jnp.int32),) + (quarter,) * 7,
        in_specs=[SMEM, pl.BlockSpec(memory_space=pltpu.HBM)],
        out_specs=(SMEM,) + (VMEM,) * 7,
        scratch_shapes=[pltpu.SemaphoreType.DMA((4,))],
        compiler_params=pltpu.CompilerParams(vmem_limit_bytes=56 * 1024 * 1024),
        name="head",
    )(pairing, block)


def tail_kernel(slots, y0, y1, y2, y3, out, sems):
    rows = y0.shape[0]
    copies = []
    for index, y in enumerate((y0, y1, y2, y3)):
        target = out.at[pl.ds(pl.multiple_of(slots[index] * rows, rows), rows)]
        copies.append(pltpu.make_async_copy(y, target, sems.at[index]))
        copies[-1].start()
    for copy in copies:
        copy.wait()


def tail(slots, pieces):
    rows = pieces[0].shape[0]
    return pl.pallas_call(
        tail_kernel,
        out_shape=jax.ShapeDtypeStruct((4 * rows, BLK), jnp.float32),
        in_specs=[SMEM] + [VMEM] * 4,
        out_specs=ANY,
        scratch_shapes=[pltpu.SemaphoreType.DMA((4,))],
        compiler_params=PARAMS,
        name="tail",
    )(slots, *pieces)


def gram_kernel(slots, own, x0, x1, x2, x3, part, high, low):
    for index, x in enumerate((x0, x1, x2, x3)):
        h, l = split(x[...])
        high[slots[index]] = h
        low[slots[index]] = l
    def keep(index, value):
        part[:, index] = value.reshape(ROWS, BLK // ROWS, BLK)

    def wide(x, a):
        return jnp.concatenate([x[a], x[a + 1]], axis=1)

    for index, (a, b) in enumerate(CROSS[:2]):
        keep(index, tdot(high[a], high[b]) + (tdot(high[a], low[b]) + tdot(low[a], high[b])))
    value = tdot(wide(high, 0), wide(high, 2)) + (
        tdot(wide(high, 0), wide(low, 2)) + tdot(wide(low, 0), wide(high, 2))
    )
    for index, (a, b) in enumerate(CROSS[2:]):
        b = b - 2
        keep(2 + index, value[a * BLK : (a + 1) * BLK, b * BLK : (b + 1) * BLK])
    part[:, len(CROSS)] = own[...].reshape(ROWS, BLK // ROWS, BLK)


def gram_cross(slots, own, pieces):
    rows = pieces[0].shape[0]
    return pl.pallas_call(
        gram_kernel,
        out_shape=(
            jax.ShapeDtypeStruct((ROWS, len(CROSS) + 1, BLK // ROWS, BLK), jnp.float32),
            jax.ShapeDtypeStruct((4, rows, BLK), jnp.bfloat16),
            jax.ShapeDtypeStruct((4, rows, BLK), jnp.bfloat16),
        ),
        in_specs=[SMEM] + [VMEM] * 5,
        out_specs=(VMEM, VMEM, VMEM),
        compiler_params=PARAMS,
        name="gram_cross",
    )(slots, own, *pieces)


def spread_kernel(a, b, c, d, out):
    count = len(CROSS)
    cross = (a[:count] + b[:count]) + (c[:count] + d[:count])
    whole = jnp.concatenate([cross] + [x[count:] for x in (a, b, c, d)])
    out[...] = jnp.broadcast_to(whole, out.shape)


def spread(parts):
    return pl.pallas_call(
        spread_kernel,
        out_shape=jax.ShapeDtypeStruct((ROWS, len(CROSS) + 4, BLK // ROWS, BLK), jnp.float32),
        in_specs=[VMEM] * 4,
        out_specs=VMEM,
        compiler_params=PARAMS,
        name="spread",
    )(*parts)


def turn_steps(gram, turn):
    row_id = lax.broadcasted_iota(jnp.int32, (BLK, BLK), 0)
    col_id = lax.broadcasted_iota(jnp.int32, (BLK, BLK), 1)
    eye = row_id == col_id
    for pair in range(2):
        unit = eye.astype(jnp.float32)
        zero = jnp.zeros((BLK, BLK), jnp.float32)
        for index, value in enumerate((unit, zero, zero, unit)):
            turn[pair, index] = value

    def diag(value):
        return jnp.sum(jnp.where(eye, value, 0.0), axis=0, keepdims=True)

    def upright(value):
        return jnp.sum(jnp.where(eye, value, 0.0), axis=1, keepdims=True)

    def back(value, axis):
        return pltpu.roll(value, BLK - 1, axis)

    def angles(ll, lr, rl, rr):
        a, g, e = diag(ll), diag(lr), diag(rr)
        gap = e - a
        sign = jnp.where(gap >= 0.0, 1.0, -1.0)
        denom = jnp.abs(gap) + jnp.sqrt(gap * gap + 4.0 * g * g) + TIE_GUARD * (a + e)
        tangent = 2.0 * g * sign / denom
        cosine = 1.0 / jnp.sqrt(1.0 + tangent * tangent)
        return cosine, cosine * tangent

    def step(_, carry):
        grams = [[gram[pair, index] for index in range(4)] for pair in range(2)]
        rows = [angles(*blocks) for blocks in grams]
        upper = [
            (ll * c - lr * s, ll * s + lr * c, rl * c - rr * s, rl * s + rr * c)
            for (ll, lr, rl, rr), (c, s) in zip(grams, rows)
        ]
        columns = [(upright(c), upright(s)) for c, s in rows]
        for pair in range(2):
            c, s = rows[pair]
            for side in (0, 2):
                left, right = turn[pair, side], turn[pair, side + 1]
                turn[pair, side] = left * c - right * s
                turn[pair, side + 1] = back(left * s + right * c, 1)
        for pair in range(2):
            (ul, ur, dl, dr), (c, s) = upper[pair], columns[pair]
            gram[pair, 0] = c * ul - s * dl
            gram[pair, 1] = back(c * ur - s * dr, 1)
            gram[pair, 2] = back(s * ul + c * dl, 0)
            gram[pair, 3] = back(back(s * ur + c * dr, 0), 1)
        return carry

    lax.fori_loop(0, SHIFTS, step, 0, unroll=2)
    for pair in range(2):
        for index in (1, 3):
            turn[pair, index] = pltpu.roll(turn[pair, index], SHIFTS, 1)
        gram[pair, 3] = pltpu.roll(pltpu.roll(gram[pair, 3], SHIFTS, 0), SHIFTS, 1)


def turn_kernel(slots, sums, out_high, out_low, gram, turn, first):
    def place(which):
        found = jnp.int32(0)
        for j in range(1, 4):
            found = jnp.where(slots[j] == which, j, found)
        return found

    def block(index):
        return sums[:, index].reshape(BLK, BLK)

    for pair in range(2):
        gram[pair, 0] = block(len(CROSS) + place(2 * pair))
        gram[pair, 1] = block(pair)
        gram[pair, 2] = block(pair).T
        gram[pair, 3] = block(len(CROSS) + place(2 * pair + 1))
    turn_steps(gram, turn)
    for pair in range(2):
        for side in range(2):
            first[pair, side, :BLK] = turn[pair, side]
            first[pair, side, BLK:] = turn[pair, 2 + side]
    both = jnp.concatenate(
        [
            jnp.concatenate([block(2), block(4)], axis=1),
            jnp.concatenate([block(5), block(3)], axis=1),
        ],
        axis=0,
    )
    left = [gram[0, 0], gram[0, 3]]
    right = [gram[1, 0], gram[1, 3]]
    for side in range(2):
        half = dot3(both, first[1, side], dot)
        mixed = dot3(first[0, side], half, tdot)
        gram[side, 0] = left[side]
        gram[side, 1] = mixed
        gram[side, 2] = mixed.T
        gram[side, 3] = right[side]
    turn_steps(gram, turn)
    for side in range(2):
        for pair in range(2):
            for late in range(2):
                value = dot3(first[pair, side], turn[side, 2 * pair + late], dot)
                h, l = split(value)
                out_high[2 * late + side, 2 * BLK * pair : 2 * BLK * (pair + 1), :] = h
                out_low[2 * late + side, 2 * BLK * pair : 2 * BLK * (pair + 1), :] = l


def turns(slots, sums):
    return pl.pallas_call(
        turn_kernel,
        out_shape=(
            jax.ShapeDtypeStruct((4, 4 * BLK, BLK), jnp.bfloat16),
            jax.ShapeDtypeStruct((4, 4 * BLK, BLK), jnp.bfloat16),
        ),
        in_specs=[SMEM, VMEM],
        out_specs=(VMEM, VMEM),
        scratch_shapes=[
            pltpu.VMEM((2, 4, BLK, BLK), jnp.float32),
            pltpu.VMEM((2, 4, BLK, BLK), jnp.float32),
            pltpu.VMEM((2, 2, 2 * BLK, BLK), jnp.float32),
        ],
        compiler_params=PARAMS,
        name="turns",
    )(slots, sums)


def apply_kernel(which, slots, high, low, w_high, w_low, *outs):
    step = 256

    def body(index, carry):
        rows = pl.ds(index * step, step)
        xh = jnp.concatenate([high[j, rows] for j in range(4)], axis=1)
        xl = jnp.concatenate([low[j, rows] for j in range(4)], axis=1)
        for j in range(0, len(which), 2):
            places = [slots[which[j]], slots[which[j + 1]]]
            wh = jnp.concatenate([w_high[p] for p in places], axis=1)
            wl = jnp.concatenate([w_low[p] for p in places], axis=1)
            value = dot(xh, wh) + (dot(xh, wl) + dot(xl, wh))
            outs[j][rows, :] = value[:, :BLK]
            outs[j + 1][rows, :] = value[:, BLK:]
        return carry

    lax.fori_loop(0, high.shape[1] // step, body, 0)


def apply_turn(slots, which, high, low, w_high, w_low):
    piece = jax.ShapeDtypeStruct(high.shape[1:], jnp.float32)
    return pl.pallas_call(
        partial(apply_kernel, which),
        out_shape=[piece] * len(which),
        in_specs=[SMEM] + [VMEM] * 4,
        out_specs=[VMEM] * len(which),
        compiler_params=PARAMS,
        name="apply_turn",
    )(slots, high, low, w_high, w_low)


def own_kernel(p0, p1, p2, p3, out):
    def product(x):
        h, l = split(x)
        return tdot(h, h) + (tdot(h, l) + tdot(l, h))

    step = 256
    out[...] = jnp.zeros((BLK, BLK), jnp.float32)

    def body(index, carry):
        total = out[...]
        for p in (p0, p1, p2, p3):
            total += product(p[pl.ds(index * step, step), :])
        out[...] = total
        return carry

    lax.fori_loop(0, p0.shape[0] // step, body, 0)


def own_gram(pieces):
    return pl.pallas_call(
        own_kernel,
        out_shape=jax.ShapeDtypeStruct((BLK, BLK), jnp.float32),
        in_specs=[VMEM] * 4,
        out_specs=VMEM,
        compiler_params=PARAMS,
        name="own_gram",
    )(*pieces)


def swap(masks, parts):
    return [lax.ppermute(x, "cols", route(m)) for x, m in zip(parts, masks)]


def gate_kernel(token, p1, p2, p3, q1, q2, q3):
    pass


def gate(token, pieces):
    return pl.pallas_call(
        gate_kernel,
        out_shape=[jax.ShapeDtypeStruct(p.shape, p.dtype) for p in pieces],
        in_specs=[VMEM] + [ANY] * 3,
        out_specs=[ANY] * 3,
        input_output_aliases={1: 0, 2: 1, 3: 2},
        compiler_params=PARAMS,
        name="gate",
    )(token, *pieces)


def bring(masks, parts, came, near, own):
    return swap(masks, parts), own


def leave(parts, came, near, own):
    return list(came), own_gram([near, *parts])


def share(masks, part):
    return swap(masks, [part] * 3)


def by_mask(which, function, *operands, other=None):
    branches = [partial(function, (u, u ^ ALL_BITS, ALL_BITS)) for u in range(1, 8)]
    if other is not None:
        branches.append(other)
    return lax.switch(which, branches, *operands)


def over_rows(x):
    return lax.all_to_all(x, "rows", split_axis=0, concat_axis=0, tiled=True)


def on_device(anomalies, pairing):
    slots, first, *rest = head(pairing, anomalies)
    which = slots[4]

    def stay(parts, came, near, own):
        return list(parts), near

    def hand_on(step, parts, came, near, own):
        token = came[0][:8] + came[1][:8] + came[2][:8]
        token = lax.ppermute(token, "cols", route(step))
        return list(gate(token, parts)), near

    def middle(parts, came, near, own):
        part, high, low = gram_cross(slots, own, [near, *came])
        part = over_rows(part).sum(axis=0)
        sums = over_rows(spread([part] + by_mask(which, share, part)))
        w_high, w_low = turns(slots, sums)
        near, *far = apply_turn(slots, (0, 1, 2, 3), high, low, w_high, w_low)
        return far, near

    def wave(number, carry):
        parts, came, near, own = carry
        code = lax.dynamic_index_in_dim(slots, 5 + number, 0, keepdims=False)
        stage, now = code >> 3, code & 7
        stages_of = [stay, partial(hand_on, 1), partial(hand_on, 2), middle]
        parts, near = lax.switch(stage, stages_of, parts, came, near, own)
        came, own = by_mask(now, bring, parts, came, near, own, other=leave)
        return parts, came, near, own

    own = jnp.zeros((BLK, BLK), jnp.float32)
    _, came, near, _ = lax.fori_loop(0, 3, wave, (rest[:3], rest[3:], first, own))
    return tail(slots, [near, *came])


def solution(mesh):
    placed = (P("rows", "cols"), P())
    return jax.shard_map(
        on_device, mesh=mesh, in_specs=placed, out_specs=P("rows", "cols"), check_vma=False
    )
```

```python
from functools import partial

import jax
import jax.numpy as jnp
from jax import lax
from jax.experimental import pallas as pl
from jax.experimental.pallas import tpu as pltpu
from jax.sharding import PartitionSpec as P

BLK = 128
SHIFTS = 8
TIE_GUARD = 1e-06
COLS = 16
ROWS = 16
ALL_BITS = COLS - 1
STAY = 7
CROSS = ((0, 1), (2, 3), (0, 2), (1, 3), (0, 3), (1, 2))
VMEM = pl.BlockSpec(memory_space=pltpu.VMEM)
SMEM = pl.BlockSpec(memory_space=pltpu.SMEM)
ANY = pl.BlockSpec(memory_space=pl.ANY)
PARAMS = pltpu.CompilerParams(vmem_limit_bytes=20 * 1024 * 1024)


def route(mask):
    return [(b, b ^ mask) for b in range(COLS)]


def split(x):
    high = x.astype(jnp.bfloat16)
    return high, (x - high.astype(jnp.float32)).astype(jnp.bfloat16)


def tdot(left, right):
    return lax.dot_general(
        left, right, (((0,), (0,)), ((), ())), preferred_element_type=jnp.float32
    )


def dot(left, right):
    return jnp.dot(left, right, preferred_element_type=jnp.float32)


def dot3(left, right, product):
    lh, ll = split(left)
    rh, rl = split(right)
    return product(lh, rh) + (product(lh, rl) + product(ll, rh))


def odd(value):
    return bin(value).count("1") % 2


def halves(small):
    step = 2 if small == 1 else 1
    fits = [
        w
        for w in range(1, COLS)
        if not any(odd(w & m) for m in (small, ALL_BITS)) and odd(w & step)
    ]
    return fits[0]


def head_kernel(pairing, block, slots, p0, p1, p2, p3, e1, e2, e3, sems):
    position = lax.axis_index("cols")
    mask = pairing[0, 0]
    late = mask ^ ALL_BITS

    def top_bit(value):
        return jnp.where(value >= 8, 8, jnp.where(value >= 4, 4, jnp.where(value >= 2, 2, 1)))

    me = jnp.where((position & top_bit(mask)) != 0, 1, 0)
    me += jnp.where((position & top_bit(late)) != 0, 2, 0)
    small = jnp.minimum(mask, late)
    code = jnp.where(mask == small, 1, 2)
    places = (me, me ^ code, me ^ (3 - code), me ^ 3)
    rows = p0.shape[0]
    copies = []
    for index, (place, piece) in enumerate(zip(places, (p0, p1, p2, p3))):
        slots[index] = place
        source = block.at[pl.ds(pl.multiple_of(place * rows, rows), rows)]
        copies.append(pltpu.make_async_copy(source, piece, sems.at[index]))
        copies[-1].start()
    half = jnp.int32(halves(1))
    for u in range(2, 8):
        half = jnp.where(small == u, halves(u), half)
    half = half & position
    half = half ^ (half >> 2)
    half = (half ^ (half >> 1)) & 1
    slots[4] = small - 1
    slots[5] = jnp.where(half == 0, small - 1, STAY)
    slots[6] = jnp.where(half == 1, small - 1, STAY) + 8 * jnp.where(small == 1, 2, 1)
    slots[7] = small - 1 + 8 * 3
    for empty in (e1, e2, e3):
        empty[:8] = jnp.zeros((8, BLK), jnp.float32)
    for copy in copies:
        copy.wait()


def head(pairing, block):
    quarter = jax.ShapeDtypeStruct((block.shape[0] // 4, BLK), jnp.float32)
    return pl.pallas_call(
        head_kernel,
        out_shape=(jax.ShapeDtypeStruct((8,), jnp.int32),) + (quarter,) * 7,
        in_specs=[SMEM, pl.BlockSpec(memory_space=pltpu.HBM)],
        out_specs=(SMEM,) + (VMEM,) * 7,
        scratch_shapes=[pltpu.SemaphoreType.DMA((4,))],
        compiler_params=pltpu.CompilerParams(vmem_limit_bytes=56 * 1024 * 1024),
        name="head",
    )(pairing, block)


def tail_kernel(slots, y0, y1, y2, y3, out, sems):
    rows = y0.shape[0]
    copies = []
    for index, y in enumerate((y0, y1, y2, y3)):
        target = out.at[pl.ds(pl.multiple_of(slots[index] * rows, rows), rows)]
        copies.append(pltpu.make_async_copy(y, target, sems.at[index]))
        copies[-1].start()
    for copy in copies:
        copy.wait()


def tail(slots, pieces):
    rows = pieces[0].shape[0]
    return pl.pallas_call(
        tail_kernel,
        out_shape=jax.ShapeDtypeStruct((4 * rows, BLK), jnp.float32),
        in_specs=[SMEM] + [VMEM] * 4,
        out_specs=ANY,
        scratch_shapes=[pltpu.SemaphoreType.DMA((4,))],
        compiler_params=PARAMS,
        name="tail",
    )(slots, *pieces)


def gram_kernel(slots, own, x0, x1, x2, x3, part, high, low):
    for index, x in enumerate((x0, x1, x2, x3)):
        h, l = split(x[...])
        high[slots[index]] = h
        low[slots[index]] = l
    def keep(index, value):
        part[:, index] = value.reshape(ROWS, BLK // ROWS, BLK)

    def wide(x, a):
        return jnp.concatenate([x[a], x[a + 1]], axis=1)

    for index, (a, b) in enumerate(CROSS[:2]):
        keep(index, tdot(high[a], high[b]) + (tdot(high[a], low[b]) + tdot(low[a], high[b])))
    value = tdot(wide(high, 0), wide(high, 2)) + (
        tdot(wide(high, 0), wide(low, 2)) + tdot(wide(low, 0), wide(high, 2))
    )
    for index, (a, b) in enumerate(CROSS[2:]):
        b = b - 2
        keep(2 + index, value[a * BLK : (a + 1) * BLK, b * BLK : (b + 1) * BLK])
    part[:, len(CROSS)] = own[...].reshape(ROWS, BLK // ROWS, BLK)


def gram_cross(slots, own, pieces):
    rows = pieces[0].shape[0]
    return pl.pallas_call(
        gram_kernel,
        out_shape=(
            jax.ShapeDtypeStruct((ROWS, len(CROSS) + 1, BLK // ROWS, BLK), jnp.float32),
            jax.ShapeDtypeStruct((4, rows, BLK), jnp.bfloat16),
            jax.ShapeDtypeStruct((4, rows, BLK), jnp.bfloat16),
        ),
        in_specs=[SMEM] + [VMEM] * 5,
        out_specs=(VMEM, VMEM, VMEM),
        compiler_params=PARAMS,
        name="gram_cross",
    )(slots, own, *pieces)


def spread_kernel(a, b, c, d, out):
    count = len(CROSS)
    cross = (a[:count] + b[:count]) + (c[:count] + d[:count])
    whole = jnp.concatenate([cross] + [x[count:] for x in (a, b, c, d)])
    out[...] = jnp.broadcast_to(whole, out.shape)


def spread(parts):
    return pl.pallas_call(
        spread_kernel,
        out_shape=jax.ShapeDtypeStruct((ROWS, len(CROSS) + 4, BLK // ROWS, BLK), jnp.float32),
        in_specs=[VMEM] * 4,
        out_specs=VMEM,
        compiler_params=PARAMS,
        name="spread",
    )(*parts)


def turn_steps(gram, turn):
    row_id = lax.broadcasted_iota(jnp.int32, (BLK, BLK), 0)
    col_id = lax.broadcasted_iota(jnp.int32, (BLK, BLK), 1)
    eye = row_id == col_id
    for pair in range(2):
        unit = eye.astype(jnp.float32)
        zero = jnp.zeros((BLK, BLK), jnp.float32)
        for index, value in enumerate((unit, zero, zero, unit)):
            turn[pair, index] = value

    def diag(value):
        return jnp.sum(jnp.where(eye, value, 0.0), axis=0, keepdims=True)

    def upright(value):
        return jnp.sum(jnp.where(eye, value, 0.0), axis=1, keepdims=True)

    def back(value, axis):
        return pltpu.roll(value, BLK - 1, axis)

    def angles(ll, lr, rl, rr):
        a, g, e = diag(ll), diag(lr), diag(rr)
        gap = e - a
        sign = jnp.where(gap >= 0.0, 1.0, -1.0)
        denom = jnp.abs(gap) + jnp.sqrt(gap * gap + 4.0 * g * g) + TIE_GUARD * (a + e)
        tangent = 2.0 * g * sign / denom
        cosine = 1.0 / jnp.sqrt(1.0 + tangent * tangent)
        return cosine, cosine * tangent

    def step(_, carry):
        grams = [[gram[pair, index] for index in range(4)] for pair in range(2)]
        rows = [angles(*blocks) for blocks in grams]
        upper = [
            (ll * c - lr * s, ll * s + lr * c, rl * c - rr * s, rl * s + rr * c)
            for (ll, lr, rl, rr), (c, s) in zip(grams, rows)
        ]
        columns = [(upright(c), upright(s)) for c, s in rows]
        for pair in range(2):
            c, s = rows[pair]
            for side in (0, 2):
                left, right = turn[pair, side], turn[pair, side + 1]
                turn[pair, side] = left * c - right * s
                turn[pair, side + 1] = back(left * s + right * c, 1)
        for pair in range(2):
            (ul, ur, dl, dr), (c, s) = upper[pair], columns[pair]
            gram[pair, 0] = c * ul - s * dl
            gram[pair, 1] = back(c * ur - s * dr, 1)
            gram[pair, 2] = back(s * ul + c * dl, 0)
            gram[pair, 3] = back(back(s * ur + c * dr, 0), 1)
        return carry

    lax.fori_loop(0, SHIFTS, step, 0, unroll=4)
    for pair in range(2):
        for index in (1, 3):
            turn[pair, index] = pltpu.roll(turn[pair, index], SHIFTS, 1)
        gram[pair, 3] = pltpu.roll(pltpu.roll(gram[pair, 3], SHIFTS, 0), SHIFTS, 1)


def turn_kernel(slots, sums, out_high, out_low, gram, turn, first):
    def place(which):
        found = jnp.int32(0)
        for j in range(1, 4):
            found = jnp.where(slots[j] == which, j, found)
        return found

    def block(index):
        return sums[:, index].reshape(BLK, BLK)

    for pair in range(2):
        gram[pair, 0] = block(len(CROSS) + place(2 * pair))
        gram[pair, 1] = block(pair)
        gram[pair, 2] = block(pair).T
        gram[pair, 3] = block(len(CROSS) + place(2 * pair + 1))
    turn_steps(gram, turn)
    for pair in range(2):
        for side in range(2):
            first[pair, side, :BLK] = turn[pair, side]
            first[pair, side, BLK:] = turn[pair, 2 + side]
    both = jnp.concatenate(
        [
            jnp.concatenate([block(2), block(4)], axis=1),
            jnp.concatenate([block(5), block(3)], axis=1),
        ],
        axis=0,
    )
    left = [gram[0, 0], gram[0, 3]]
    right = [gram[1, 0], gram[1, 3]]
    for side in range(2):
        half = dot3(both, first[1, side], dot)
        mixed = dot3(first[0, side], half, tdot)
        gram[side, 0] = left[side]
        gram[side, 1] = mixed
        gram[side, 2] = mixed.T
        gram[side, 3] = right[side]
    turn_steps(gram, turn)
    for side in range(2):
        for pair in range(2):
            for late in range(2):
                value = dot3(first[pair, side], turn[side, 2 * pair + late], dot)
                h, l = split(value)
                out_high[2 * late + side, 2 * BLK * pair : 2 * BLK * (pair + 1), :] = h
                out_low[2 * late + side, 2 * BLK * pair : 2 * BLK * (pair + 1), :] = l


def turns(slots, sums):
    return pl.pallas_call(
        turn_kernel,
        out_shape=(
            jax.ShapeDtypeStruct((4, 4 * BLK, BLK), jnp.bfloat16),
            jax.ShapeDtypeStruct((4, 4 * BLK, BLK), jnp.bfloat16),
        ),
        in_specs=[SMEM, VMEM],
        out_specs=(VMEM, VMEM),
        scratch_shapes=[
            pltpu.VMEM((2, 4, BLK, BLK), jnp.float32),
            pltpu.VMEM((2, 4, BLK, BLK), jnp.float32),
            pltpu.VMEM((2, 2, 2 * BLK, BLK), jnp.float32),
        ],
        compiler_params=PARAMS,
        name="turns",
    )(slots, sums)


def apply_kernel(which, slots, high, low, w_high, w_low, *outs):
    step = 512

    def body(index, carry):
        rows = pl.ds(index * step, step)
        xh = jnp.concatenate([high[j, rows] for j in range(4)], axis=1)
        xl = jnp.concatenate([low[j, rows] for j in range(4)], axis=1)
        for j in range(0, len(which), 2):
            places = [slots[which[j]], slots[which[j + 1]]]
            wh = jnp.concatenate([w_high[p] for p in places], axis=1)
            wl = jnp.concatenate([w_low[p] for p in places], axis=1)
            value = dot(xh, wh) + (dot(xh, wl) + dot(xl, wh))
            outs[j][rows, :] = value[:, :BLK]
            outs[j + 1][rows, :] = value[:, BLK:]
        return carry

    lax.fori_loop(0, high.shape[1] // step, body, 0)


def apply_turn(slots, which, high, low, w_high, w_low):
    piece = jax.ShapeDtypeStruct(high.shape[1:], jnp.float32)
    return pl.pallas_call(
        partial(apply_kernel, which),
        out_shape=[piece] * len(which),
        in_specs=[SMEM] + [VMEM] * 4,
        out_specs=[VMEM] * len(which),
        compiler_params=PARAMS,
        name="apply_turn",
    )(slots, high, low, w_high, w_low)


def own_kernel(p0, p1, p2, p3, out):
    def product(x):
        h, l = split(x)
        return tdot(h, h) + (tdot(h, l) + tdot(l, h))

    step = 256
    out[...] = jnp.zeros((BLK, BLK), jnp.float32)

    def body(index, carry):
        total = out[...]
        for p in (p0, p1, p2, p3):
            total += product(p[pl.ds(index * step, step), :])
        out[...] = total
        return carry

    lax.fori_loop(0, p0.shape[0] // step, body, 0)


def own_gram(pieces):
    return pl.pallas_call(
        own_kernel,
        out_shape=jax.ShapeDtypeStruct((BLK, BLK), jnp.float32),
        in_specs=[VMEM] * 4,
        out_specs=VMEM,
        compiler_params=PARAMS,
        name="own_gram",
    )(*pieces)


def swap(masks, parts):
    return [lax.ppermute(x, "cols", route(m)) for x, m in zip(parts, masks)]


def gate_kernel(token, p1, p2, p3, q1, q2, q3):
    pass


def gate(token, pieces):
    return pl.pallas_call(
        gate_kernel,
        out_shape=[jax.ShapeDtypeStruct(p.shape, p.dtype) for p in pieces],
        in_specs=[VMEM] + [ANY] * 3,
        out_specs=[ANY] * 3,
        input_output_aliases={1: 0, 2: 1, 3: 2},
        compiler_params=PARAMS,
        name="gate",
    )(token, *pieces)


def bring(masks, parts, came, near, own):
    return swap(masks, parts), own


def leave(parts, came, near, own):
    return list(came), own_gram([near, *parts])


def share(masks, part):
    return swap(masks, [part] * 3)


def by_mask(which, function, *operands, other=None):
    branches = [partial(function, (u, u ^ ALL_BITS, ALL_BITS)) for u in range(1, 8)]
    if other is not None:
        branches.append(other)
    return lax.switch(which, branches, *operands)


def over_rows(x):
    return lax.all_to_all(x, "rows", split_axis=0, concat_axis=0, tiled=True)


def on_device(anomalies, pairing):
    slots, first, *rest = head(pairing, anomalies)

    def stay(now, parts, came, near, own):
        return list(parts), near

    def hand_on(step, now, parts, came, near, own):
        token = came[0][:8] + came[1][:8] + came[2][:8]
        token = lax.ppermute(token, "cols", route(step))
        return list(gate(token, parts)), near

    def middle(now, parts, came, near, own):
        part, high, low = gram_cross(slots, own, [near, *came])
        part = over_rows(part).sum(axis=0)
        sums = over_rows(spread([part] + by_mask(now, share, part)))
        w_high, w_low = turns(slots, sums)
        near, *far = apply_turn(slots, (0, 1, 2, 3), high, low, w_high, w_low)
        return far, near

    def wave(number, carry):
        parts, came, near, own = carry
        code = lax.dynamic_index_in_dim(slots, 5 + number, 0, keepdims=False)
        stage, now = code >> 3, code & 7
        stages_of = [stay, partial(hand_on, 1), partial(hand_on, 2), middle]
        parts, near = lax.switch(stage, stages_of, now, parts, came, near, own)
        came, own = by_mask(now, bring, parts, came, near, own, other=leave)
        return parts, came, near, own

    own = jnp.zeros((BLK, BLK), jnp.float32)
    _, came, near, _ = lax.fori_loop(0, 3, wave, (rest[:3], rest[3:], first, own))
    return tail(slots, [near, *came])


def solution(mesh):
    placed = (P("rows", "cols"), P())
    return jax.shard_map(
        on_device, mesh=mesh, in_specs=placed, out_specs=P("rows", "cols"), check_vma=False
    )
```

```python
from functools import partial

import jax
import jax.numpy as jnp
from jax import lax
from jax.experimental import pallas as pl
from jax.experimental.pallas import tpu as pltpu
from jax.sharding import PartitionSpec as P

BLK = 128
SHIFTS = 8
TIE_GUARD = 1e-06
COLS = 16
ROWS = 16
ALL_BITS = COLS - 1
STAY = 7
CROSS = ((0, 1), (2, 3), (0, 2), (1, 3), (0, 3), (1, 2))
VMEM = pl.BlockSpec(memory_space=pltpu.VMEM)
SMEM = pl.BlockSpec(memory_space=pltpu.SMEM)
ANY = pl.BlockSpec(memory_space=pl.ANY)
PARAMS = pltpu.CompilerParams(vmem_limit_bytes=20 * 1024 * 1024)


def route(mask):
    return [(b, b ^ mask) for b in range(COLS)]


def split(x):
    high = x.astype(jnp.bfloat16)
    return high, (x - high.astype(jnp.float32)).astype(jnp.bfloat16)


def tdot(left, right):
    return lax.dot_general(
        left, right, (((0,), (0,)), ((), ())), preferred_element_type=jnp.float32
    )


def dot(left, right):
    return jnp.dot(left, right, preferred_element_type=jnp.float32)


def dot3(left, right, product):
    lh, ll = split(left)
    rh, rl = split(right)
    return product(lh, rh) + (product(lh, rl) + product(ll, rh))


def odd(value):
    return bin(value).count("1") % 2


def halves(small):
    step = 2 if small == 1 else 1
    fits = [
        w
        for w in range(1, COLS)
        if not any(odd(w & m) for m in (small, ALL_BITS)) and odd(w & step)
    ]
    return fits[0]


def head_kernel(pairing, block, slots, p0, p1, p2, p3, e1, e2, e3, sems):
    position = lax.axis_index("cols")
    mask = pairing[0, 0]
    late = mask ^ ALL_BITS

    def top_bit(value):
        return jnp.where(value >= 8, 8, jnp.where(value >= 4, 4, jnp.where(value >= 2, 2, 1)))

    me = jnp.where((position & top_bit(mask)) != 0, 1, 0)
    me += jnp.where((position & top_bit(late)) != 0, 2, 0)
    small = jnp.minimum(mask, late)
    code = jnp.where(mask == small, 1, 2)
    places = (me, me ^ code, me ^ (3 - code), me ^ 3)
    rows = p0.shape[0]
    copies = []
    for index, (place, piece) in enumerate(zip(places, (p0, p1, p2, p3))):
        slots[index] = place
        source = block.at[pl.ds(pl.multiple_of(place * rows, rows), rows)]
        copies.append(pltpu.make_async_copy(source, piece, sems.at[index]))
        copies[-1].start()
    half = jnp.int32(halves(1))
    for u in range(2, 8):
        half = jnp.where(small == u, halves(u), half)
    half = half & position
    half = half ^ (half >> 2)
    half = (half ^ (half >> 1)) & 1
    slots[4] = small - 1
    slots[5] = jnp.where(half == 0, small - 1, STAY)
    slots[6] = jnp.where(half == 1, small - 1, STAY) + 8 * jnp.where(small == 1, 2, 1)
    slots[7] = small - 1 + 8 * 3
    for empty in (e1, e2, e3):
        empty[:8] = jnp.zeros((8, BLK), jnp.float32)
    for copy in copies:
        copy.wait()


def head(pairing, block):
    quarter = jax.ShapeDtypeStruct((block.shape[0] // 4, BLK), jnp.float32)
    return pl.pallas_call(
        head_kernel,
        out_shape=(jax.ShapeDtypeStruct((8,), jnp.int32),) + (quarter,) * 7,
        in_specs=[SMEM, pl.BlockSpec(memory_space=pltpu.HBM)],
        out_specs=(SMEM,) + (VMEM,) * 7,
        scratch_shapes=[pltpu.SemaphoreType.DMA((4,))],
        compiler_params=pltpu.CompilerParams(vmem_limit_bytes=56 * 1024 * 1024),
        name="head",
    )(pairing, block)


def tail_kernel(slots, y0, y1, y2, y3, out, sems):
    rows = y0.shape[0]
    copies = []
    for index, y in enumerate((y0, y1, y2, y3)):
        target = out.at[pl.ds(pl.multiple_of(slots[index] * rows, rows), rows)]
        copies.append(pltpu.make_async_copy(y, target, sems.at[index]))
        copies[-1].start()
    for copy in copies:
        copy.wait()


def tail(slots, pieces):
    rows = pieces[0].shape[0]
    return pl.pallas_call(
        tail_kernel,
        out_shape=jax.ShapeDtypeStruct((4 * rows, BLK), jnp.float32),
        in_specs=[SMEM] + [VMEM] * 4,
        out_specs=ANY,
        scratch_shapes=[pltpu.SemaphoreType.DMA((4,))],
        compiler_params=PARAMS,
        name="tail",
    )(slots, *pieces)


def gram_kernel(slots, own, x0, x1, x2, x3, part, high, low):
    for index, x in enumerate((x0, x1, x2, x3)):
        h, l = split(x[...])
        high[slots[index]] = h
        low[slots[index]] = l
    def keep(index, value):
        part[:, index] = value.reshape(ROWS, BLK // ROWS, BLK)

    def wide(x, a):
        return jnp.concatenate([x[a], x[a + 1]], axis=1)

    for index, (a, b) in enumerate(CROSS[:2]):
        keep(index, tdot(high[a], high[b]) + (tdot(high[a], low[b]) + tdot(low[a], high[b])))
    value = tdot(wide(high, 0), wide(high, 2)) + (
        tdot(wide(high, 0), wide(low, 2)) + tdot(wide(low, 0), wide(high, 2))
    )
    for index, (a, b) in enumerate(CROSS[2:]):
        b = b - 2
        keep(2 + index, value[a * BLK : (a + 1) * BLK, b * BLK : (b + 1) * BLK])
    part[:, len(CROSS)] = own[...].reshape(ROWS, BLK // ROWS, BLK)


def gram_cross(slots, own, pieces):
    rows = pieces[0].shape[0]
    return pl.pallas_call(
        gram_kernel,
        out_shape=(
            jax.ShapeDtypeStruct((ROWS, len(CROSS) + 1, BLK // ROWS, BLK), jnp.float32),
            jax.ShapeDtypeStruct((4, rows, BLK), jnp.bfloat16),
            jax.ShapeDtypeStruct((4, rows, BLK), jnp.bfloat16),
        ),
        in_specs=[SMEM] + [VMEM] * 5,
        out_specs=(VMEM, VMEM, VMEM),
        compiler_params=PARAMS,
        name="gram_cross",
    )(slots, own, *pieces)


def spread_kernel(a, b, c, d, out):
    count = len(CROSS)
    cross = (a[:count] + b[:count]) + (c[:count] + d[:count])
    whole = jnp.concatenate([cross] + [x[count:] for x in (a, b, c, d)])
    out[...] = jnp.broadcast_to(whole, out.shape)


def spread(parts):
    return pl.pallas_call(
        spread_kernel,
        out_shape=jax.ShapeDtypeStruct((ROWS, len(CROSS) + 4, BLK // ROWS, BLK), jnp.float32),
        in_specs=[VMEM] * 4,
        out_specs=VMEM,
        compiler_params=PARAMS,
        name="spread",
    )(*parts)


def turn_steps(gram, turn):
    row_id = lax.broadcasted_iota(jnp.int32, (BLK, BLK), 0)
    col_id = lax.broadcasted_iota(jnp.int32, (BLK, BLK), 1)
    eye = row_id == col_id
    for pair in range(2):
        unit = eye.astype(jnp.float32)
        zero = jnp.zeros((BLK, BLK), jnp.float32)
        for index, value in enumerate((unit, zero, zero, unit)):
            turn[pair, index] = value

    def diag(value):
        return jnp.sum(jnp.where(eye, value, 0.0), axis=0, keepdims=True)

    def upright(value):
        return jnp.sum(jnp.where(eye, value, 0.0), axis=1, keepdims=True)

    def back(value, axis):
        return pltpu.roll(value, BLK - 1, axis)

    def angles(ll, lr, rl, rr):
        a, g, e = diag(ll), diag(lr), diag(rr)
        gap = e - a
        sign = jnp.where(gap >= 0.0, 1.0, -1.0)
        denom = jnp.abs(gap) + jnp.sqrt(gap * gap + 4.0 * g * g) + TIE_GUARD * (a + e)
        tangent = 2.0 * g * sign / denom
        cosine = 1.0 / jnp.sqrt(1.0 + tangent * tangent)
        return cosine, cosine * tangent

    def step(_, carry):
        grams = [[gram[pair, index] for index in range(4)] for pair in range(2)]
        rows = [angles(*blocks) for blocks in grams]
        upper = [
            (ll * c - lr * s, ll * s + lr * c, rl * c - rr * s, rl * s + rr * c)
            for (ll, lr, rl, rr), (c, s) in zip(grams, rows)
        ]
        columns = [(upright(c), upright(s)) for c, s in rows]
        for pair in range(2):
            c, s = rows[pair]
            for side in (0, 2):
                left, right = turn[pair, side], turn[pair, side + 1]
                turn[pair, side] = left * c - right * s
                turn[pair, side + 1] = back(left * s + right * c, 1)
        for pair in range(2):
            (ul, ur, dl, dr), (c, s) = upper[pair], columns[pair]
            gram[pair, 0] = c * ul - s * dl
            gram[pair, 1] = back(c * ur - s * dr, 1)
            gram[pair, 2] = back(s * ul + c * dl, 0)
            gram[pair, 3] = back(back(s * ur + c * dr, 0), 1)
        return carry

    lax.fori_loop(0, SHIFTS, step, 0, unroll=8)
    for pair in range(2):
        for index in (1, 3):
            turn[pair, index] = pltpu.roll(turn[pair, index], SHIFTS, 1)
        gram[pair, 3] = pltpu.roll(pltpu.roll(gram[pair, 3], SHIFTS, 0), SHIFTS, 1)


def turn_kernel(slots, sums, out_high, out_low, gram, turn, first):
    def place(which):
        found = jnp.int32(0)
        for j in range(1, 4):
            found = jnp.where(slots[j] == which, j, found)
        return found

    def block(index):
        return sums[:, index].reshape(BLK, BLK)

    for pair in range(2):
        gram[pair, 0] = block(len(CROSS) + place(2 * pair))
        gram[pair, 1] = block(pair)
        gram[pair, 2] = block(pair).T
        gram[pair, 3] = block(len(CROSS) + place(2 * pair + 1))
    turn_steps(gram, turn)
    for pair in range(2):
        for side in range(2):
            first[pair, side, :BLK] = turn[pair, side]
            first[pair, side, BLK:] = turn[pair, 2 + side]
    both = jnp.concatenate(
        [
            jnp.concatenate([block(2), block(4)], axis=1),
            jnp.concatenate([block(5), block(3)], axis=1),
        ],
        axis=0,
    )
    left = [gram[0, 0], gram[0, 3]]
    right = [gram[1, 0], gram[1, 3]]
    for side in range(2):
        half = dot3(both, first[1, side], dot)
        mixed = dot3(first[0, side], half, tdot)
        gram[side, 0] = left[side]
        gram[side, 1] = mixed
        gram[side, 2] = mixed.T
        gram[side, 3] = right[side]
    turn_steps(gram, turn)
    for side in range(2):
        for pair in range(2):
            for late in range(2):
                value = dot3(first[pair, side], turn[side, 2 * pair + late], dot)
                h, l = split(value)
                out_high[2 * late + side, 2 * BLK * pair : 2 * BLK * (pair + 1), :] = h
                out_low[2 * late + side, 2 * BLK * pair : 2 * BLK * (pair + 1), :] = l


def turns(slots, sums):
    return pl.pallas_call(
        turn_kernel,
        out_shape=(
            jax.ShapeDtypeStruct((4, 4 * BLK, BLK), jnp.bfloat16),
            jax.ShapeDtypeStruct((4, 4 * BLK, BLK), jnp.bfloat16),
        ),
        in_specs=[SMEM, VMEM],
        out_specs=(VMEM, VMEM),
        scratch_shapes=[
            pltpu.VMEM((2, 4, BLK, BLK), jnp.float32),
            pltpu.VMEM((2, 4, BLK, BLK), jnp.float32),
            pltpu.VMEM((2, 2, 2 * BLK, BLK), jnp.float32),
        ],
        compiler_params=PARAMS,
        name="turns",
    )(slots, sums)


def apply_kernel(which, slots, high, low, w_high, w_low, *outs):
    step = 512

    def body(index, carry):
        rows = pl.ds(index * step, step)
        xh = jnp.concatenate([high[j, rows] for j in range(4)], axis=1)
        xl = jnp.concatenate([low[j, rows] for j in range(4)], axis=1)
        for j in range(0, len(which), 2):
            places = [slots[which[j]], slots[which[j + 1]]]
            wh = jnp.concatenate([w_high[p] for p in places], axis=1)
            wl = jnp.concatenate([w_low[p] for p in places], axis=1)
            value = dot(xh, wh) + (dot(xh, wl) + dot(xl, wh))
            outs[j][rows, :] = value[:, :BLK]
            outs[j + 1][rows, :] = value[:, BLK:]
        return carry

    lax.fori_loop(0, high.shape[1] // step, body, 0)


def apply_turn(slots, which, high, low, w_high, w_low):
    piece = jax.ShapeDtypeStruct(high.shape[1:], jnp.float32)
    return pl.pallas_call(
        partial(apply_kernel, which),
        out_shape=[piece] * len(which),
        in_specs=[SMEM] + [VMEM] * 4,
        out_specs=[VMEM] * len(which),
        compiler_params=PARAMS,
        name="apply_turn",
    )(slots, high, low, w_high, w_low)


def own_kernel(p0, p1, p2, p3, out):
    def product(x):
        h, l = split(x)
        return tdot(h, h) + (tdot(h, l) + tdot(l, h))

    step = 256
    out[...] = jnp.zeros((BLK, BLK), jnp.float32)

    def body(index, carry):
        total = out[...]
        for p in (p0, p1, p2, p3):
            total += product(p[pl.ds(index * step, step), :])
        out[...] = total
        return carry

    lax.fori_loop(0, p0.shape[0] // step, body, 0)


def own_gram(pieces):
    return pl.pallas_call(
        own_kernel,
        out_shape=jax.ShapeDtypeStruct((BLK, BLK), jnp.float32),
        in_specs=[VMEM] * 4,
        out_specs=VMEM,
        compiler_params=PARAMS,
        name="own_gram",
    )(*pieces)


def swap(masks, parts):
    return [lax.ppermute(x, "cols", route(m)) for x, m in zip(parts, masks)]


def gate_kernel(token, p1, p2, p3, q1, q2, q3):
    pass


def gate(token, pieces):
    return pl.pallas_call(
        gate_kernel,
        out_shape=[jax.ShapeDtypeStruct(p.shape, p.dtype) for p in pieces],
        in_specs=[VMEM] + [ANY] * 3,
        out_specs=[ANY] * 3,
        input_output_aliases={1: 0, 2: 1, 3: 2},
        compiler_params=PARAMS,
        name="gate",
    )(token, *pieces)


def bring(masks, parts, came, near, own):
    return swap(masks, parts), own


def leave(parts, came, near, own):
    return list(came), own_gram([near, *parts])


def share(masks, part):
    return swap(masks, [part] * 3)


def by_mask(which, function, *operands, other=None):
    branches = [partial(function, (u, u ^ ALL_BITS, ALL_BITS)) for u in range(1, 8)]
    if other is not None:
        branches.append(other)
    return lax.switch(which, branches, *operands)


def over_rows(x):
    return lax.all_to_all(x, "rows", split_axis=0, concat_axis=0, tiled=True)


def on_device(anomalies, pairing):
    slots, first, *rest = head(pairing, anomalies)

    def stay(now, parts, came, near, own):
        return list(parts), near

    def hand_on(step, now, parts, came, near, own):
        token = came[0][:8] + came[1][:8] + came[2][:8]
        token = lax.ppermute(token, "cols", route(step))
        return list(gate(token, parts)), near

    def middle(now, parts, came, near, own):
        part, high, low = gram_cross(slots, own, [near, *came])
        part = over_rows(part).sum(axis=0)
        sums = over_rows(spread([part] + by_mask(now, share, part)))
        w_high, w_low = turns(slots, sums)
        near, *far = apply_turn(slots, (0, 1, 2, 3), high, low, w_high, w_low)
        return far, near

    def wave(number, carry):
        parts, came, near, own = carry
        code = lax.dynamic_index_in_dim(slots, 5 + number, 0, keepdims=False)
        stage, now = code >> 3, code & 7
        stages_of = [stay, partial(hand_on, 1), partial(hand_on, 2), middle]
        parts, near = lax.switch(stage, stages_of, now, parts, came, near, own)
        came, own = by_mask(now, bring, parts, came, near, own, other=leave)
        return parts, came, near, own

    own = jnp.zeros((BLK, BLK), jnp.float32)
    _, came, near, _ = lax.fori_loop(0, 3, wave, (rest[:3], rest[3:], first, own))
    return tail(slots, [near, *came])


def solution(mesh):
    placed = (P("rows", "cols"), P())
    return jax.shard_map(
        on_device, mesh=mesh, in_specs=placed, out_specs=P("rows", "cols"), check_vma=False
    )
```
